512 devices in a mesh: grp: 8 (over y), sub: 64 (over z, x, core).
Axes of the slice: x: 4, y: 8, z: 8, core: 2. Of those that a mesh axis runs over, the one named last changes fastest.
Arguments:
- coupling: bfloat16 [16384, 192, 192], P(('grp', 'sub')), may hold values from -0.4375 to 0.4375
- factors: bfloat16 [2048, 192, 192], P(('grp', 'sub'))
- face_diag: float32 [16384, 192], P(('grp', 'sub')), may hold values from 4 to 16
- face_block: int32 [16384], P(('grp', 'sub')), may hold values from 0 to 3
- face_owner: int32 [16384, 1], P(('grp', 'sub')), may hold values from 0 to 63; in each aligned block of 32 rows (0 to 31, 32 to 63, ...) at most 2 rows name the same one
- owner_slot: int32 [16384], P(('grp', 'sub')), may hold values from 0 to 11
- coarse_basis: bfloat16 [6144, 192, 128], P(('grp', 'sub')), may hold values from -0.03125 to 0.03125
- coarse_index: int32 [65536], P(('grp', 'sub')), may hold values from 0 to 767, as said below
- projection: bfloat16 [6144, 256], P('grp'), may hold values from -1 to 1
Outputs:
- owned_schur: bfloat16 [6144, 192, 192], P(('grp', 'sub'))
- top_coarse: float32 [256, 256], replicated
The draws below stay inside these ranges and needn't reach their ends.
Inputs may be any that keep to these rules, and one draw needn't show every extreme that they name: `face_owner`: among the faces of one subdomain no owner is named more than 2 times, and some subdomain names some owner exactly 2 times. `coarse_index`: the 128 entries of one subdomain are distinct.
All inputs are finite; a program needn't handle non-finite values.
Results may differ from the reference program's by a relative error of at most 0.0034.
Values may be sent and summed in bfloat16 or wider, within the bound.
No kernel may reach another device: no remote copies, remote signals or barrier semaphores. Data moves between devices by JAX's collectives and lax.ppermute only.
A program may use at most 128 MiB of HBM per device.

```python
import math
import jax
import jax.numpy as jnp
import numpy as np
from jax import lax

FW = 192
NE = 4
OWNF = 12
CAP = 2
NCL = 128
NCG = 768
NCT = 256
NFD = 32
SUBS = 512
N_GRP = 8
N_SUB = 64


def draw_factors(key, part):
    key = jax.random.fold_in(key, 11)
    key_diag, key_noise = jax.random.split(key)
    diag_vals = jax.random.uniform(key_diag, (SUBS * NE, FW), jnp.float32, 1.0, 2.0)
    noise = jax.random.normal(key_noise, (SUBS * NE, FW, FW), jnp.float32) * (0.5 / FW ** 0.5)
    identity = jnp.eye(FW, dtype=jnp.float32)
    return (noise + diag_vals[:, :, None] * identity).astype(jnp.bfloat16)


def pick_window(sub_key, sub_id):
    offsets = jax.random.permutation(sub_key, 2 * NCL)[:NCL].astype(jnp.int32)
    return (offsets + sub_id * (NCG // N_SUB)) % NCG


def draw_coarse_index(key, part):
    key = jax.random.fold_in(key, 23)
    keys = jax.random.split(key, SUBS)
    sub_ids = jnp.arange(SUBS, dtype=jnp.int32) % N_SUB
    chosen = jax.vmap(pick_window)(keys, sub_ids)
    return chosen.reshape(SUBS * NCL).astype(jnp.int32)


def draw_projection(key, part):
    key = jax.random.fold_in(key, 31)
    total_rows = N_GRP * NCG
    noise = jax.random.truncated_normal(key, -4.0, 4.0, (total_rows, NCT), jnp.float32) * (NCG * 8) ** (-0.5)
    row_ids = jnp.arange(total_rows, dtype=jnp.int32)[:, None]
    col_ids = jnp.arange(NCT, dtype=jnp.int32)[None, :]
    home_col = row_ids * NCT // total_rows
    amplitude = (NCT / total_rows) ** 0.5
    return (noise + jnp.where(home_col == col_ids, amplitude, 0.0)).astype(jnp.bfloat16)


def set_ends(array, key, least, top_value):
    extent = array.shape
    place = [jax.random.randint(jax.random.fold_in(key, axis), (), 0, extent[axis]) for axis in range(len(extent))]
    array = array.at[tuple(place)].set(least)
    longest = extent.index(max(extent))
    place[longest] = (place[longest] + 1) % extent[longest]
    return array.at[tuple(place)].set(top_value)


def level_of(stream_key, shape, shards, low, top_value):
    gain, own = 1.0, jax.random.fold_in(stream_key, 6)
    for axis_at, shards_of in shards:
        draws = jnp.exp(jax.random.uniform(jax.random.fold_in(own, axis_at), (shards_of,), jnp.float32, low / len(shards), top_value / len(shards)))
        gain = gain * jnp.repeat(draws, shape[axis_at] // shards_of).reshape([-1 if axis == axis_at else 1 for axis in range(len(shape))])
    return gain


def assign_block(key, own, number, rows, count, top, limit, slope):
    sequence = jax.random.permutation(key, count)
    packed, ordinary = load_shares(count, rows * top, limit, slope, True), load_shares(count, rows * top, limit, slope, False)
    places = jnp.arange(count)

    def named(tallies, offset_by):
        used = int((tallies > 0).sum())
        fixed = max(1, used // 4)
        moved = fixed + (places - fixed + offset_by * (used - fixed)) % max(1, count - fixed)
        return jnp.zeros((count,), jnp.int32).at[sequence[jnp.where(places < fixed, places, moved)]].set(jnp.asarray(tallies, jnp.int32))

    tallies = jnp.where(number % 4 == 0, named(packed, number // 4), named(ordinary, number - number // 4 - 1))
    mixed = jax.random.permutation(jax.random.fold_in(own, 3), count)
    donor, sink = mixed[0:count // 2 * 2:2], mixed[1:count // 2 * 2:2]
    margin = jnp.minimum(tallies[donor] - 1, limit - tallies[sink]) // 2
    margin = jnp.where((donor == sequence[0]) | (sink == sequence[0]) | (tallies[sink] == 0), 0, jnp.maximum(margin, 0))
    moved = jax.random.randint(jax.random.fold_in(own, 4), (count // 2,), 0, 1 << 20) % (margin + 1)
    tallies = tallies.at[donor].add(-moved).at[sink].add(moved)
    labels = jnp.searchsorted(jnp.cumsum(tallies), jnp.arange(rows * top), side="right").astype(jnp.int32)
    listing = labels.reshape(top, rows).T
    listing = listing[jax.random.permutation(jax.random.fold_in(own, 1), rows)]
    offset_by = jax.random.randint(jax.random.fold_in(own, 2), (rows, 1), 0, top)
    return jnp.take_along_axis(listing, (jnp.arange(top)[None, :] + offset_by) % top, axis=1)


def load_shares(number_of, total, limit, slope, full):
    weights = [(1 << 20) // math.isqrt(grade ** slope) + 1 for grade in range(1, number_of + 1)]
    largest = limit if full else min(limit, max(-(-total // number_of), total * weights[0] // sum(weights)))
    least = 1 if total - largest >= number_of - 1 else 0
    given, spare = [largest] + [least] * (number_of - 1), total - largest - least * (number_of - 1)
    while spare > 0:
        free = [i for i in range(1, number_of) if given[i] < largest] or [i for i in range(1, number_of) if given[i] < limit]
        pool, left = sum([weights[i] for i in free]), spare
        for i in free:
            extra = min(limit - given[i], max(1, left * weights[i] // pool), spare)
            given[i] = given[i] + extra
            spare = spare - extra
    return np.array(given)


def normal_values(rng, shape, deviation, limit, shards=(), kind=jnp.bfloat16):
    level = level_of(rng, shape, shards, -0.22, 0.18) if shards else 1.0
    entries = jax.random.normal(rng, shape, jnp.float32) * deviation * level
    return jnp.minimum(jnp.maximum(entries, -limit), limit).astype(kind)


def setup_inputs(seed: int = 0) -> dict:
    streams_of = jax.random.split(jax.random.key(seed), 10)
    coupling = normal_values(streams_of[0], (SUBS * NFD, FW, FW), FW ** -0.5, 0.4375, ((0, 512),))
    factors = draw_factors(jax.random.fold_in(streams_of[9], 71), 0)
    face_diag = jnp.clip(jnp.exp(math.log(16.0) - 1.3862944 * jax.random.uniform(streams_of[2], (SUBS * NFD, FW), jnp.float32) ** level_of(streams_of[2], (SUBS * NFD, FW), ((0, 512),), -0.2, 0.2)), 4.0, 16.0)
    face_block = set_ends(jax.random.randint(streams_of[3], (SUBS * NFD,), 0, NE), jax.random.fold_in(streams_of[3], 1), 0, NE - 1).astype(jnp.int32)
    face_owner_keys = jax.random.split(jax.random.fold_in(streams_of[4], 1), (SUBS * NFD) // NFD)
    face_owner_turns = jax.random.permutation(jax.random.fold_in(streams_of[4], 3), (SUBS * NFD) // NFD)
    face_owner = jax.vmap(lambda own, number: assign_block(jax.random.fold_in(streams_of[4], 2), own, number, NFD, N_SUB, 1, CAP, 2))(face_owner_keys, face_owner_turns).reshape((SUBS * NFD, 1))
    owner_slot = set_ends(jax.random.randint(streams_of[5], (SUBS * NFD,), 0, OWNF), jax.random.fold_in(streams_of[5], 1), 0, OWNF - 1).astype(jnp.int32)
    coarse_basis = normal_values(streams_of[6], (SUBS * OWNF, FW, NCL), (FW * OWNF * 16) ** -0.5, 0.03125, ((0, 512),))
    coarse_index = draw_coarse_index(jax.random.fold_in(streams_of[9], 71), 0)
    projection = draw_projection(jax.random.fold_in(streams_of[9], 71), 0)
    return dict(coupling=coupling, factors=factors, face_diag=face_diag, face_block=face_block, face_owner=face_owner, owner_slot=owner_slot, coarse_basis=coarse_basis, coarse_index=coarse_index, projection=projection)


def face_schur(coupling, factors, face_diag, face_block):
    picked = factors[face_block].astype(jnp.float32)
    interior = jnp.einsum("fij,fjk->fik", picked, coupling.astype(jnp.float32))
    interior = lax.optimization_barrier(interior.astype(jnp.bfloat16)).astype(jnp.float32)
    correction = jnp.einsum("fij,fik->fjk", interior, interior)
    identity = jnp.eye(FW, dtype=jnp.float32)
    schur = (face_diag[:, :, None] * identity - correction).astype(jnp.bfloat16)
    return lax.optimization_barrier(schur).astype(jnp.float32)


def group_work(inputs):
    coupling_g, factors_g, diag_g, block_g, owner_g, slot_g, basis_g, index_g, proj_g = inputs

    def visit(running, entry_set):
        coupling_d, factors_d, diag_d, block_d, owner_d, slot_d = entry_set
        schur = face_schur(coupling_d, factors_d, diag_d, block_d)
        targets = (owner_d * OWNF + slot_d).astype(jnp.int32)
        return running.at[targets].add(schur), None

    initial = jnp.zeros((N_SUB * OWNF, FW, FW), jnp.float32)
    running, unused = lax.scan(visit, initial, (coupling_g, factors_g, diag_g, block_g, owner_g, slot_g))
    assembled = lax.optimization_barrier(running.astype(jnp.bfloat16))
    owned_f = assembled.astype(jnp.float32).reshape(N_SUB, OWNF, FW, FW)
    basis_f = basis_g.astype(jnp.float32)
    applied = jnp.einsum("dsij,dsjc->dsic", owned_f, basis_f)
    applied = lax.optimization_barrier(applied.astype(jnp.bfloat16)).astype(jnp.float32)
    local_coarse = jnp.einsum("dsic,dsie->dce", basis_f, applied)
    group_matrix = jnp.zeros((NCG, NCG), jnp.float32).at[index_g[:, :, None], index_g[:, None, :]].add(local_coarse)
    proj_f = proj_g.astype(jnp.float32)
    projected = jnp.dot(group_matrix, proj_f, precision=lax.Precision.HIGHEST)
    top_part = jnp.dot(proj_f.T, projected, precision=lax.Precision.HIGHEST)
    return top_part, assembled


def reference(coupling, factors, face_diag, face_block, face_owner, owner_slot, coarse_basis, coarse_index, projection):
    inputs = (
        coupling.reshape(N_GRP, N_SUB, NFD, FW, FW),
        factors.reshape(N_GRP, N_SUB, NE, FW, FW),
        face_diag.reshape(N_GRP, N_SUB, NFD, FW),
        face_block.reshape(N_GRP, N_SUB, NFD).astype(jnp.int32),
        face_owner.reshape(N_GRP, N_SUB, NFD).astype(jnp.int32),
        owner_slot.reshape(N_GRP, N_SUB, NFD).astype(jnp.int32),
        coarse_basis.reshape(N_GRP, N_SUB, OWNF, FW, NCL),
        coarse_index.reshape(N_GRP, N_SUB, NCL).astype(jnp.int32),
        projection.reshape(N_GRP, NCG, NCT),
    )
    top_parts, assembled = lax.map(group_work, inputs)
    return assembled.reshape(SUBS * OWNF, FW, FW), jnp.sum(top_parts, axis=0)
```

```python
import jax
import jax.numpy as jnp
from jax import lax
from jax.experimental import pallas as pl
from jax.experimental.pallas import tpu as pltpu
from jax.sharding import PartitionSpec as P

Q = 64
LANES = 128
STEP_FACES = 8
KEEP, OWNER_AT, SLOT_AT = 63, 61, 60
VMEM_LIMIT = 56 * 1024 * 1024
f32, bf16, i32 = jnp.float32, jnp.bfloat16, jnp.int32


def masks():
    row = lax.broadcasted_iota(i32, (Q, LANES), 0)
    lane = lax.broadcasted_iota(i32, (Q, LANES), 1)
    d = ((lane & (Q - 1)) - row) & (Q - 1)
    keep = (d < Q // 2) | ((d == Q // 2) & (row < Q // 2))
    return lane < Q, d, keep


def swap_halves(x):
    return pltpu.roll(x, Q, 1)


def schur_kernel(block_ref, owner_ref, slot_ref, coupling_ref, factors_ref, diag_ref, out_ref, scratch):
    step = pl.program_id(0)
    left, d, keep = masks()
    eye = d == 0
    pairs = out_ref.shape[1] // 5
    for pair in range(STEP_FACES // 2):
        last = None
        for odd in range(2):
            q = pair * 2 + odd
            face = step * STEP_FACES + q
            c = coupling_ref[q]
            mid = c[:, Q : 2 * Q]
            columns = jnp.concatenate([c[:, 2 * Q :], mid, mid, c[:, :Q]], axis=1)
            interior = jnp.dot(
                factors_ref[block_ref[face]], columns, preferred_element_type=f32
            ).astype(bf16)
            g = lax.dot_general(
                interior, interior, (((0,), (0,)), ((), ())), preferred_element_type=f32
            )
            d3, r1 = g[:Q, :LANES], g[Q : 2 * Q, :LANES]
            t0, d1 = g[3 * Q :, :LANES], g[3 * Q :, LANES:]
            diag01 = diag_ref[q : q + 1, :LANES]
            diag2 = jnp.concatenate([diag_ref[q : q + 1, LANES:]] * 2, axis=1)
            t1 = jnp.where(eye & ~left, swap_halves(diag01), 0.0) - jnp.where(
                left | ~keep, r1, d1
            )
            d2_diag = jnp.sum(
                jnp.where(eye & ~left, diag01 - r1, 0.0), axis=1, keepdims=True
            )
            spare = jnp.where(
                d == KEEP,
                d2_diag,
                jnp.where(
                    d == OWNER_AT,
                    owner_ref[face].astype(f32),
                    jnp.where(d == SLOT_AT, slot_ref[face].astype(f32), 0.0),
                ),
            )
            f = jnp.where(keep, jnp.where(eye, diag2, 0.0) - d3, spare)
            at = step * (STEP_FACES // 2) + pair

            def put(k, value):
                scratch[pl.ds(k * Q * pairs + at, Q, stride=pairs), :] = value

            put(2 * odd, -t0)
            put(2 * odd + 1, t1)
            if odd:
                put(4, jnp.where(left, last, swap_halves(f)))
            last = f

    @pl.when(step == pl.num_programs(0) - 1)
    def _():
        for k in range(5):
            out_ref[:, pairs * k : pairs * (k + 1), :] = (
                scratch[Q * pairs * k : Q * pairs * (k + 1), :]
                .reshape(Q, pairs, LANES)
                .astype(bf16)
            )


def pack_faces(face_block, owner, slot, coupling, factors, face_diag):
    faces, width, _ = coupling.shape
    blocks = factors.shape[0]
    pairs = faces // 2
    return pl.pallas_call(
        schur_kernel,
        grid_spec=pltpu.PrefetchScalarGridSpec(
            num_scalar_prefetch=3,
            grid=(faces // STEP_FACES,),
            in_specs=[
                pl.BlockSpec((STEP_FACES, width, width), lambda s, *_: (s, 0, 0)),
                pl.BlockSpec((blocks, width, width), lambda s, *_: (0, 0, 0)),
                pl.BlockSpec((STEP_FACES, width), lambda s, *_: (s, 0)),
            ],
            out_specs=pl.BlockSpec((Q, 5 * pairs, LANES), lambda s, *_: (0, 0, 0)),
            scratch_shapes=[pltpu.VMEM((5 * Q * pairs, LANES), f32)],
        ),
        out_shape=jax.ShapeDtypeStruct((Q, 5 * pairs, LANES), bf16),
        compiler_params=pltpu.CompilerParams(vmem_limit_bytes=VMEM_LIMIT),
        name="pack_faces",
    )(face_block, owner, slot, coupling, factors, face_diag)


def merge_kernel(me_ref, x_ref, out_ref, flat):
    peers, rows, _ = x_ref.shape
    pairs = rows // 5
    total = peers * pairs
    slots = 12
    me = me_ref[0]

    def piece(k):
        return x_ref[:, pairs * k : pairs * (k + 1), :].reshape(total, LANES)

    shared = piece(4)
    which = lax.broadcasted_iota(i32, (8, LANES), 0)
    lane = lax.broadcasted_iota(i32, (8, LANES), 1)
    place = ((me + jnp.where((which & 1) == 0, OWNER_AT, SLOT_AT)) & (Q - 1)) + jnp.where(
        which < 2, 0, Q
    )
    pick = ((lane == place) & (which < 4)).astype(f32).astype(bf16)
    named = lax.dot_general(
        pick, shared, (((1,), (1,)), ((), ())), preferred_element_type=f32
    ).astype(i32)
    target = lax.broadcasted_iota(i32, (slots * peers, total), 0)
    even = (target == named[1:2] * peers + named[0:1]).astype(f32).astype(bf16)
    odd = (target == named[3:4] * peers + named[2:3]).astype(f32).astype(bf16)
    sums = []
    for k in range(2):
        sums.append(
            jnp.dot(even, piece(k), preferred_element_type=f32)
            + jnp.dot(odd, piece(2 + k), preferred_element_type=f32)
        )
    low = jnp.dot(even, shared, preferred_element_type=f32)
    high = jnp.dot(odd, shared, preferred_element_type=f32)
    half = slots // 2
    first = half * peers
    left = lax.broadcasted_iota(i32, (first, LANES), 1) < Q
    sums.append(
        jnp.where(
            left,
            low[:first] + swap_halves(high[:first]),
            swap_halves(low[first:]) + high[first:],
        )
    )
    out_rows = out_ref.shape[1]
    for k in range(3):
        for s in range(sums[k].shape[0] // peers):
            flat[pl.ds(slots * k + s, peers, stride=out_rows), :] = sums[k][
                peers * s : peers * (s + 1), :
            ]
    for s in range(slots * 2 + half, out_rows):
        flat[pl.ds(s, peers, stride=out_rows), :] = jnp.zeros((peers, LANES), f32)
    out_ref[...] = flat[...].reshape(peers, out_rows, LANES).astype(bf16)


def merge_rows(me, x):
    peers = x.shape[0]
    return pl.pallas_call(
        merge_kernel,
        in_specs=[
            pl.BlockSpec(memory_space=pltpu.SMEM),
            pl.BlockSpec(memory_space=pltpu.VMEM),
        ],
        out_specs=pl.BlockSpec(memory_space=pltpu.VMEM),
        scratch_shapes=[pltpu.VMEM((peers * 32, LANES), f32)],
        out_shape=jax.ShapeDtypeStruct((peers, 32, LANES), bf16),
        compiler_params=pltpu.CompilerParams(vmem_limit_bytes=VMEM_LIMIT),
        name="merge_rows",
    )(me, x)


def split3(x):
    a = x.astype(bf16)
    rest = x - a.astype(f32)
    b = rest.astype(bf16)
    return a, b, (rest - b.astype(f32)).astype(bf16)


def coarse_kernel(z_ref, basis_ref, rows_ref, owned_ref, top_ref, flat, applied):
    slots, width, coarse = basis_ref.shape
    half = slots // 2
    step = z_ref.shape[1]
    left, d, keep = masks()
    eye = d == 0
    flat[...] = z_ref[...].reshape(Q * step, LANES).astype(f32)
    for q in range(half):
        f_both = flat[pl.ds(slots * 2 + q, Q, stride=step), :]
        f_turned = f_both.T
        for r in (q, q + half):
            t0 = flat[pl.ds(r, Q, stride=step), :]
            t1 = flat[pl.ds(slots + r, Q, stride=step), :]
            turned = jnp.concatenate([t0, t1], axis=0).T
            lower = turned[Q:]
            if r == q:
                f, f_t = f_both, f_turned[:Q]
            else:
                f, f_t = swap_halves(f_both), f_turned[Q:]
            d2_diag = jnp.sum(
                jnp.where((d == KEEP) & left, f, 0.0), axis=1, keepdims=True
            )
            d1 = swap_halves(jnp.where(keep, t1, lower))
            d2 = jnp.where(eye, d2_diag, jnp.where(keep, lower, t1))
            d3 = jnp.where(keep[:, :Q], f[:, :Q], f_t)
            owned_ref[r, :Q, :LANES] = jnp.where(left, d1, t0).astype(bf16)
            owned_ref[r, :Q, LANES:] = t0[:, :Q].astype(bf16)
            owned_ref[r, Q : 2 * Q, :LANES] = jnp.where(left, lower, d2).astype(bf16)
            owned_ref[r, Q : 2 * Q, LANES:] = t1[:, :Q].astype(bf16)
            owned_ref[r, 2 * Q :, :LANES] = turned[:Q].astype(bf16)
            owned_ref[r, 2 * Q :, LANES:] = d3.astype(bf16)
    for r in range(slots):
        applied[r] = jnp.dot(
            owned_ref[r], basis_ref[r], preferred_element_type=f32
        ).astype(bf16)
    local_coarse = lax.dot_general(
        basis_ref[...].reshape(slots * width, coarse),
        applied[...].reshape(slots * width, coarse),
        (((0,), (0,)), ((), ())),
        preferred_element_type=f32,
    )
    rows_t = rows_ref[...]
    inner = 0.0
    for part in split3(local_coarse):
        inner += lax.dot_general(
            part, rows_t, (((1,), (1,)), ((), ())), preferred_element_type=f32
        )
    top = 0.0
    for part in split3(inner):
        top += jnp.dot(rows_t, part, preferred_element_type=f32)
    size = top.shape[0]
    for k in range(size // LANES):
        top_ref[size * k : size * (k + 1), :] = top[:, LANES * k : LANES * (k + 1)]


def owned_and_top(z, basis, rows_t):
    slots, width, coarse = basis.shape
    size = rows_t.shape[0]
    vmem = pl.BlockSpec(memory_space=pltpu.VMEM)
    return pl.pallas_call(
        coarse_kernel,
        in_specs=[vmem, vmem, vmem],
        out_specs=[vmem, vmem],
        scratch_shapes=[
            pltpu.VMEM((Q * z.shape[1], LANES), f32),
            pltpu.VMEM((slots, width, coarse), bf16),
        ],
        out_shape=[
            jax.ShapeDtypeStruct((slots, width, width), bf16),
            jax.ShapeDtypeStruct((size * size // LANES, LANES), f32),
        ],
        compiler_params=pltpu.CompilerParams(vmem_limit_bytes=VMEM_LIMIT),
        name="owned_and_top",
    )(z, basis, rows_t)


def exchange(x, axis):
    return lax.all_to_all(x, axis, split_axis=0, concat_axis=0, tiled=True)


def local(
    coupling,
    factors,
    face_diag,
    face_block,
    face_owner,
    owner_slot,
    coarse_basis,
    coarse_index,
    projection,
):
    peers, groups = lax.axis_size("sub"), lax.axis_size("grp")
    me = lax.axis_index("sub").astype(i32).reshape(1)
    x = pack_faces(face_block, face_owner[:, 0], owner_slot, coupling, factors, face_diag)
    x = exchange(x, "sub")
    group_size, size = projection.shape
    placement = (coarse_index[:, None] == lax.iota(i32, group_size)[None, :]).astype(bf16)
    rows_t = lax.dot_general(
        projection, placement, (((0,), (1,)), ((), ())), preferred_element_type=f32
    ).astype(bf16)
    z = exchange(merge_rows(me, x), "sub")
    owned, top = owned_and_top(z, coarse_basis, rows_t)
    share = size * size // LANES // peers
    part = jnp.sum(exchange(top.reshape(peers, share, LANES), "sub"), axis=0)
    part = jnp.sum(
        exchange(jnp.broadcast_to(part, (groups, share, LANES)), "grp"), axis=0
    )
    full = exchange(jnp.broadcast_to(part, (peers, share, LANES)), "sub")
    full = full.reshape(size // LANES, size, LANES)
    top_matrix = jnp.concatenate([full[k] for k in range(size // LANES)], axis=1)
    return owned, top_matrix


def solution(mesh):
    return jax.shard_map(
        local,
        mesh=mesh,
        in_specs=(
            P(("grp", "sub"), None, None),
            P(("grp", "sub"), None, None),
            P(("grp", "sub"), None),
            P(("grp", "sub")),
            P(("grp", "sub"), None),
            P(("grp", "sub")),
            P(("grp", "sub"), None, None),
            P(("grp", "sub")),
            P("grp", None),
        ),
        out_specs=(P(("grp", "sub"), None, None), P()),
        check_vma=False,
    )
```

```python
import jax
import jax.numpy as jnp
from jax import lax
from jax.experimental import pallas as pl
from jax.experimental.pallas import tpu as pltpu
from jax.sharding import PartitionSpec as P

Q = 64
LANES = 128
STEP_FACES = 16
KEEP, OWNER_AT, SLOT_AT = 63, 61, 60
PACK_VMEM = 56 * 1024 * 1024
VMEM_LIMIT = 16 * 1024 * 1024
f32, bf16, i32 = jnp.float32, jnp.bfloat16, jnp.int32


def masks():
    row = lax.broadcasted_iota(i32, (Q, LANES), 0)
    lane = lax.broadcasted_iota(i32, (Q, LANES), 1)
    d = ((lane & (Q - 1)) - row) & (Q - 1)
    keep = (d < Q // 2) | ((d == Q // 2) & (row < Q // 2))
    return lane < Q, d, keep


def swap_halves(x):
    return pltpu.roll(x, Q, 1)


def schur_kernel(block_ref, owner_ref, slot_ref, coupling_ref, factors_ref, diag_ref, out_ref, scratch):
    step = pl.program_id(0)
    left, d, keep = masks()
    eye = d == 0
    eye_right = eye & ~left
    pairs = out_ref.shape[1] // 5
    interiors = []
    for q in range(STEP_FACES):
        c = coupling_ref[q]
        mid = c[:, Q : 2 * Q]
        columns = jnp.concatenate([c[:, 2 * Q :], mid, mid, c[:, :Q]], axis=1)
        face = step * STEP_FACES + q
        interiors.append(
            jnp.dot(
                factors_ref[block_ref[face]], columns, preferred_element_type=f32
            ).astype(bf16)
        )
    grams = [
        lax.dot_general(x, x, (((0,), (0,)), ((), ())), preferred_element_type=f32)
        for x in interiors
    ]
    for pair in range(STEP_FACES // 2):
        last = None
        for odd in range(2):
            q = pair * 2 + odd
            face = step * STEP_FACES + q
            g = grams[q]
            d3, r1 = g[:Q, :LANES], g[Q : 2 * Q, :LANES]
            t0, d1 = g[3 * Q :, :LANES], g[3 * Q :, LANES:]
            diag01 = diag_ref[q : q + 1, :LANES]
            diag2 = jnp.concatenate([diag_ref[q : q + 1, LANES:]] * 2, axis=1)
            t1 = jnp.where(eye_right, swap_halves(diag01), 0.0) - jnp.where(
                left | ~keep, r1, d1
            )
            d2_diag = jnp.sum(
                jnp.where(eye_right, diag01 - r1, 0.0), axis=1, keepdims=True
            )
            spare = jnp.where(
                d == KEEP,
                d2_diag,
                jnp.where(
                    d == OWNER_AT,
                    owner_ref[face].astype(f32),
                    jnp.where(d == SLOT_AT, slot_ref[face].astype(f32), 0.0),
                ),
            )
            f = jnp.where(keep, jnp.where(eye, diag2, 0.0) - d3, spare)
            at = step * (STEP_FACES // 2) + pair

            def put(k, value):
                scratch[pl.ds(k * Q * pairs + at, Q, stride=pairs), :] = value

            put(2 * odd, -t0)
            put(2 * odd + 1, t1)
            if odd:
                put(4, jnp.where(left, last, swap_halves(f)))
            last = f

    @pl.when(step == pl.num_programs(0) - 1)
    def _():
        for k in range(5):
            out_ref[:, pairs * k : pairs * (k + 1), :] = (
                scratch[Q * pairs * k : Q * pairs * (k + 1), :]
                .reshape(Q, pairs, LANES)
                .astype(bf16)
            )


def pack_faces(face_block, owner, slot, coupling, factors, face_diag):
    faces, width, _ = coupling.shape
    blocks = factors.shape[0]
    pairs = faces // 2
    return pl.pallas_call(
        schur_kernel,
        grid_spec=pltpu.PrefetchScalarGridSpec(
            num_scalar_prefetch=3,
            grid=(faces // STEP_FACES,),
            in_specs=[
                pl.BlockSpec((STEP_FACES, width, width), lambda s, *_: (s, 0, 0)),
                pl.BlockSpec((blocks, width, width), lambda s, *_: (0, 0, 0)),
                pl.BlockSpec((STEP_FACES, width), lambda s, *_: (s, 0)),
            ],
            out_specs=pl.BlockSpec((Q, 5 * pairs, LANES), lambda s, *_: (0, 0, 0)),
            scratch_shapes=[pltpu.VMEM((5 * Q * pairs, LANES), f32)],
        ),
        out_shape=jax.ShapeDtypeStruct((Q, 5 * pairs, LANES), bf16),
        compiler_params=pltpu.CompilerParams(vmem_limit_bytes=PACK_VMEM),
        name="pack_faces",
    )(face_block, owner, slot, coupling, factors, face_diag)


def merge_kernel(me_ref, x_ref, out_ref, flat):
    peers, rows, _ = x_ref.shape
    pairs = rows // 5
    total = peers * pairs
    slots = 12
    me = me_ref[0]

    def piece(k):
        return x_ref[:, pairs * k : pairs * (k + 1), :].reshape(total, LANES)

    shared = piece(4)
    which = lax.broadcasted_iota(i32, (8, LANES), 0)
    lane = lax.broadcasted_iota(i32, (8, LANES), 1)
    place = ((me + jnp.where((which & 1) == 0, OWNER_AT, SLOT_AT)) & (Q - 1)) + jnp.where(
        which < 2, 0, Q
    )
    pick = ((lane == place) & (which < 4)).astype(f32).astype(bf16)
    named = lax.dot_general(
        pick, shared, (((1,), (1,)), ((), ())), preferred_element_type=f32
    ).astype(i32)
    target = lax.broadcasted_iota(i32, (slots * peers, total), 0)
    even = (target == named[1:2] * peers + named[0:1]).astype(f32).astype(bf16)
    odd = (target == named[3:4] * peers + named[2:3]).astype(f32).astype(bf16)
    sums = []
    for k in range(2):
        sums.append(
            jnp.dot(even, piece(k), preferred_element_type=f32)
            + jnp.dot(odd, piece(2 + k), preferred_element_type=f32)
        )
    low = jnp.dot(even, shared, preferred_element_type=f32)
    high = jnp.dot(odd, shared, preferred_element_type=f32)
    half = slots // 2
    first = half * peers
    left = lax.broadcasted_iota(i32, (first, LANES), 1) < Q
    sums.append(
        jnp.where(
            left,
            low[:first] + swap_halves(high[:first]),
            swap_halves(low[first:]) + high[first:],
        )
    )
    out_rows = out_ref.shape[1]
    for k in range(3):
        for s in range(sums[k].shape[0] // peers):
            flat[pl.ds(slots * k + s, peers, stride=out_rows), :] = sums[k][
                peers * s : peers * (s + 1), :
            ]
    for s in range(slots * 2 + half, out_rows):
        flat[pl.ds(s, peers, stride=out_rows), :] = jnp.zeros((peers, LANES), f32)
    out_ref[...] = flat[...].reshape(peers, out_rows, LANES).astype(bf16)


def merge_rows(me, x):
    peers = x.shape[0]
    return pl.pallas_call(
        merge_kernel,
        in_specs=[
            pl.BlockSpec(memory_space=pltpu.SMEM),
            pl.BlockSpec(memory_space=pltpu.VMEM),
        ],
        out_specs=pl.BlockSpec(memory_space=pltpu.VMEM),
        scratch_shapes=[pltpu.VMEM((peers * 32, LANES), f32)],
        out_shape=jax.ShapeDtypeStruct((peers, 32, LANES), bf16),
        compiler_params=pltpu.CompilerParams(vmem_limit_bytes=VMEM_LIMIT),
        name="merge_rows",
    )(me, x)


def split3(x):
    a = x.astype(bf16)
    rest = x - a.astype(f32)
    b = rest.astype(bf16)
    return a, b, (rest - b.astype(f32)).astype(bf16)


def coarse_kernel(z_ref, basis_ref, rows_ref, owned_ref, top_ref, flat, applied):
    slots, width, coarse = basis_ref.shape
    half = slots // 2
    step = z_ref.shape[1]
    left, d, keep = masks()
    eye = d == 0
    flat[...] = z_ref[...].reshape(Q * step, LANES).astype(f32)
    for q in range(half):
        f_both = flat[pl.ds(slots * 2 + q, Q, stride=step), :]
        f_turned = f_both.T
        for r in (q, q + half):
            t0 = flat[pl.ds(r, Q, stride=step), :]
            t1 = flat[pl.ds(slots + r, Q, stride=step), :]
            turned = jnp.concatenate([t0, t1], axis=0).T
            lower = turned[Q:]
            if r == q:
                f, f_t = f_both, f_turned[:Q]
            else:
                f, f_t = swap_halves(f_both), f_turned[Q:]
            d2_diag = jnp.sum(
                jnp.where((d == KEEP) & left, f, 0.0), axis=1, keepdims=True
            )
            d1 = swap_halves(jnp.where(keep, t1, lower))
            d2 = jnp.where(eye, d2_diag, jnp.where(keep, lower, t1))
            d3 = jnp.where(keep[:, :Q], f[:, :Q], f_t)
            owned_ref[r, :Q, :LANES] = jnp.where(left, d1, t0).astype(bf16)
            owned_ref[r, :Q, LANES:] = t0[:, :Q].astype(bf16)
            owned_ref[r, Q : 2 * Q, :LANES] = jnp.where(left, lower, d2).astype(bf16)
            owned_ref[r, Q : 2 * Q, LANES:] = t1[:, :Q].astype(bf16)
            owned_ref[r, 2 * Q :, :LANES] = turned[:Q].astype(bf16)
            owned_ref[r, 2 * Q :, LANES:] = d3.astype(bf16)
    for r in range(slots):
        applied[r] = jnp.dot(
            owned_ref[r], basis_ref[r], preferred_element_type=f32
        ).astype(bf16)
    local_coarse = lax.dot_general(
        basis_ref[...].reshape(slots * width, coarse),
        applied[...].reshape(slots * width, coarse),
        (((0,), (0,)), ((), ())),
        preferred_element_type=f32,
    )
    rows_t = rows_ref[...]
    inner = 0.0
    for part in split3(local_coarse):
        inner += lax.dot_general(
            part, rows_t, (((1,), (1,)), ((), ())), preferred_element_type=f32
        )
    upper = lower = 0.0
    for part in split3(inner):
        upper += jnp.dot(rows_t[:LANES], part, preferred_element_type=f32)
        lower += jnp.dot(rows_t[LANES:], part[:, LANES:], preferred_element_type=f32)
    top_ref[:LANES, :] = upper[:, :LANES]
    top_ref[LANES : 2 * LANES, :] = upper[:, LANES:]
    top_ref[2 * LANES :, :] = lower


def owned_and_top(z, basis, rows_t):
    slots, width, coarse = basis.shape
    vmem = pl.BlockSpec(memory_space=pltpu.VMEM)
    return pl.pallas_call(
        coarse_kernel,
        in_specs=[vmem, vmem, vmem],
        out_specs=[vmem, vmem],
        scratch_shapes=[
            pltpu.VMEM((Q * z.shape[1], LANES), f32),
            pltpu.VMEM((slots, width, coarse), bf16),
        ],
        out_shape=[
            jax.ShapeDtypeStruct((slots, width, width), bf16),
            jax.ShapeDtypeStruct((3 * LANES, LANES), f32),
        ],
        compiler_params=pltpu.CompilerParams(vmem_limit_bytes=VMEM_LIMIT),
        name="owned_and_top",
    )(z, basis, rows_t)


def mirror_kernel(x_ref, out_ref):
    mid = x_ref[LANES : 2 * LANES, :]
    out_ref[:LANES, :LANES] = x_ref[:LANES, :]
    out_ref[:LANES, LANES:] = mid
    out_ref[LANES:, :LANES] = mid.T
    out_ref[LANES:, LANES:] = x_ref[2 * LANES :, :]


def mirror(x):
    return pl.pallas_call(
        mirror_kernel,
        in_specs=[pl.BlockSpec(memory_space=pltpu.VMEM)],
        out_specs=pl.BlockSpec(memory_space=pltpu.VMEM),
        out_shape=jax.ShapeDtypeStruct((2 * LANES, 2 * LANES), f32),
        compiler_params=pltpu.CompilerParams(vmem_limit_bytes=VMEM_LIMIT),
        name="mirror",
    )(x)


def exchange(x, axis, members=None):
    return lax.all_to_all(
        x, axis, split_axis=0, concat_axis=0, tiled=True, axis_index_groups=members
    )


def sum_over_all(x, axes):
    peers, groups = (lax.axis_size(a) for a in axes[::-1])
    near = 16
    near_members = [[k * near + i for i in range(near)] for k in range(peers // near)]
    far_members = [
        list(range(i, peers * groups, near)) for i in range(near)
    ]
    far = peers * groups // near
    rows = x.shape[0] // near
    x = x.reshape(near, rows, LANES).astype(f32)
    x = jnp.sum(exchange(x, "sub", near_members).astype(f32), axis=0).astype(bf16)
    x = exchange(jnp.broadcast_to(x, (far, rows, LANES)), axes, far_members)
    x = jnp.sum(x.astype(f32), axis=0).astype(f32)
    x = exchange(jnp.broadcast_to(x, (near, rows, LANES)), "sub", near_members)
    return x.reshape(near * rows, LANES).astype(f32)


def local(
    coupling,
    factors,
    face_diag,
    face_block,
    face_owner,
    owner_slot,
    coarse_basis,
    coarse_index,
    projection,
):
    me = lax.axis_index("sub").astype(i32).reshape(1)
    x = pack_faces(face_block, face_owner[:, 0], owner_slot, coupling, factors, face_diag)
    x = exchange(x, "sub")
    group_size = projection.shape[0]
    placement = (coarse_index[:, None] == lax.iota(i32, group_size)[None, :]).astype(bf16)
    rows_t = lax.dot_general(
        projection, placement, (((0,), (1,)), ((), ())), preferred_element_type=f32
    ).astype(bf16)
    z = exchange(merge_rows(me, x), "sub")
    owned, top = owned_and_top(z, coarse_basis, rows_t)
    return owned, mirror(sum_over_all(top, ("grp", "sub")))


def solution(mesh):
    return jax.shard_map(
        local,
        mesh=mesh,
        in_specs=(
            P(("grp", "sub"), None, None),
            P(("grp", "sub"), None, None),
            P(("grp", "sub"), None),
            P(("grp", "sub")),
            P(("grp", "sub"), None),
            P(("grp", "sub")),
            P(("grp", "sub"), None, None),
            P(("grp", "sub")),
            P("grp", None),
        ),
        out_specs=(P(("grp", "sub"), None, None), P()),
        check_vma=False,
    )
```

```python
import jax
import jax.numpy as jnp
from jax import lax
from jax.experimental import pallas as pl
from jax.experimental.pallas import tpu as pltpu
from jax.sharding import PartitionSpec as P

Q = 64
LANES = 128
STEP_FACES = 16
KEEP, OWNER_AT, SLOT_AT = 63, 61, 60
PACK_VMEM = 56 * 1024 * 1024
VMEM_LIMIT = 16 * 1024 * 1024
f32, bf16, i32 = jnp.float32, jnp.bfloat16, jnp.int32


def masks():
    row = lax.broadcasted_iota(i32, (Q, LANES), 0)
    lane = lax.broadcasted_iota(i32, (Q, LANES), 1)
    d = ((lane & (Q - 1)) - row) & (Q - 1)
    keep = (d < Q // 2) | ((d == Q // 2) & (row < Q // 2))
    return lane < Q, d, keep


def swap_halves(x):
    return pltpu.roll(x, Q, 1)


def schur_kernel(
    block_hbm,
    owner_hbm,
    slot_hbm,
    coupling_hbm,
    factors_hbm,
    diag_hbm,
    out_ref,
    scratch,
    coupling_ref,
    factors_ref,
    diag_ref,
    block_ref,
    owner_ref,
    slot_ref,
    sems,
):
    faces = coupling_ref.shape[0]
    steps = faces // STEP_FACES
    pairs = faces // 2
    copies = [
        pltpu.make_async_copy(block_hbm, block_ref, sems.at[0]),
        pltpu.make_async_copy(factors_hbm, factors_ref, sems.at[1]),
    ]
    for s in range(steps):
        part = pl.ds(s * STEP_FACES, STEP_FACES)
        copies.append(
            pltpu.make_async_copy(
                coupling_hbm.at[part], coupling_ref.at[part], sems.at[2 + s]
            )
        )
    copies += [
        pltpu.make_async_copy(diag_hbm, diag_ref, sems.at[2 + steps]),
        pltpu.make_async_copy(owner_hbm, owner_ref, sems.at[3 + steps]),
        pltpu.make_async_copy(slot_hbm, slot_ref, sems.at[4 + steps]),
    ]
    for copy in copies:
        copy.start()
    left, d, keep = masks()
    eye = d == 0
    eye_right = eye & ~left
    copies[0].wait()
    copies[1].wait()
    for s in range(steps):
        copies[2 + s].wait()
        interiors = []
        for face in range(s * STEP_FACES, (s + 1) * STEP_FACES):
            c = coupling_ref[face]
            mid = c[:, Q : 2 * Q]
            columns = jnp.concatenate([c[:, 2 * Q :], mid, mid, c[:, :Q]], axis=1)
            interiors.append(
                jnp.dot(
                    factors_ref[block_ref[face]], columns, preferred_element_type=f32
                ).astype(bf16)
            )
        grams = [
            lax.dot_general(x, x, (((0,), (0,)), ((), ())), preferred_element_type=f32)
            for x in interiors
        ]
        if s == 0:
            for copy in copies[-3:]:
                copy.wait()
        last = None
        for q, g in enumerate(grams):
            face = s * STEP_FACES + q
            d3, r1 = g[:Q, :LANES], g[Q : 2 * Q, :LANES]
            t0, d1 = g[3 * Q :, :LANES], g[3 * Q :, LANES:]
            diag01 = diag_ref[face : face + 1, :LANES]
            diag2 = jnp.concatenate([diag_ref[face : face + 1, LANES:]] * 2, axis=1)
            diag10 = swap_halves(diag01)
            t1 = jnp.where(eye_right, diag10, 0.0) - jnp.where(
                left | ~keep, r1, d1
            )
            r2 = g[Q : 2 * Q, LANES:]
            d2_diag = diag10 - pltpu.roll(r2, 1, 0)
            spare = jnp.where(
                d == KEEP,
                d2_diag,
                jnp.where(
                    d == OWNER_AT,
                    owner_ref[face].astype(f32),
                    jnp.where(d == SLOT_AT, slot_ref[face].astype(f32), 0.0),
                ),
            )
            f = jnp.where(keep, jnp.where(eye, diag2, 0.0) - d3, spare)

            def put(k, value):
                scratch[pl.ds(k * Q * (pairs + 1) + face // 2, Q, stride=pairs + 1), :] = value

            odd = face % 2
            put(2 * odd, -t0)
            put(2 * odd + 1, t1)
            if odd:
                put(4, jnp.where(left, last, swap_halves(f)))
            last = f
    for k in range(5):
        for j in range(Q):
            at = Q * (pairs + 1) * k + (pairs + 1) * j
            out_ref[j, pairs * k : pairs * (k + 1), :] = scratch[at : at + pairs, :].astype(bf16)


def pack_faces(face_block, owner, slot, coupling, factors, face_diag):
    faces = coupling.shape[0]
    pairs = faces // 2
    return pl.pallas_call(
        schur_kernel,
        in_specs=[pl.BlockSpec(memory_space=pl.ANY)] * 6,
        out_specs=pl.BlockSpec(memory_space=pltpu.VMEM),
        scratch_shapes=[
            pltpu.VMEM((5 * Q * (pairs + 1), LANES), f32),
            pltpu.VMEM(coupling.shape, bf16),
            pltpu.VMEM(factors.shape, bf16),
            pltpu.VMEM(face_diag.shape, f32),
            pltpu.SMEM((faces,), i32),
            pltpu.SMEM((faces,), i32),
            pltpu.SMEM((faces,), i32),
            pltpu.SemaphoreType.DMA((5 + faces // STEP_FACES,)),
        ],
        out_shape=jax.ShapeDtypeStruct((Q, 5 * pairs, LANES), bf16),
        compiler_params=pltpu.CompilerParams(vmem_limit_bytes=PACK_VMEM),
        name="pack_faces",
    )(face_block, owner, slot, coupling, factors, face_diag)


def merge_kernel(me_ref, x_ref, out_ref, flat):
    peers, rows, _ = x_ref.shape
    pairs = rows // 5
    total = peers * pairs
    slots = 12
    me = me_ref[0]

    def piece(k):
        return x_ref[:, pairs * k : pairs * (k + 1), :].reshape(total, LANES)

    shared = piece(4)
    which = lax.broadcasted_iota(i32, (8, LANES), 0)
    lane = lax.broadcasted_iota(i32, (8, LANES), 1)
    place = ((me + jnp.where((which & 1) == 0, OWNER_AT, SLOT_AT)) & (Q - 1)) + jnp.where(
        which < 2, 0, Q
    )
    pick = ((lane == place) & (which < 4)).astype(f32).astype(bf16)
    named = lax.dot_general(
        pick, shared, (((1,), (1,)), ((), ())), preferred_element_type=f32
    ).astype(i32)
    owners = lax.broadcasted_iota(i32, (peers, total), 0)
    hots = []
    for k in range(2):
        owner_hot = (owners == named[2 * k : 2 * k + 1]).astype(f32).astype(bf16)
        slot = named[2 * k + 1 : 2 * k + 2]
        hots.append(
            jnp.concatenate(
                [owner_hot * (slot == s).astype(f32).astype(bf16) for s in range(slots)],
                axis=0,
            )
        )
    even, odd = hots
    both = jnp.dot(
        even, jnp.concatenate([piece(0), piece(1)], axis=1), preferred_element_type=f32
    ) + jnp.dot(
        odd, jnp.concatenate([piece(2), piece(3)], axis=1), preferred_element_type=f32
    )
    sums = [both[:, :LANES], both[:, LANES:]]
    low = jnp.dot(even, shared, preferred_element_type=f32)
    high = jnp.dot(odd, shared, preferred_element_type=f32)
    half = slots // 2
    first = half * peers
    left = lax.broadcasted_iota(i32, (first, LANES), 1) < Q
    sums.append(
        jnp.where(
            left,
            low[:first] + swap_halves(high[:first]),
            swap_halves(low[first:]) + high[first:],
        )
    )
    out_rows = out_ref.shape[1]
    for k in range(3):
        for s in range(sums[k].shape[0] // peers):
            flat[pl.ds(slots * k + s, peers, stride=out_rows + 1), :] = sums[k][
                peers * s : peers * (s + 1), :
            ]
    for s in range(slots * 2 + half, out_rows):
        flat[pl.ds(s, peers, stride=out_rows + 1), :] = jnp.zeros((peers, LANES), f32)
    for j in range(peers):
        at = (out_rows + 1) * j
        out_ref[j] = flat[at : at + out_rows, :].astype(bf16)


def merge_rows(me, x):
    peers = x.shape[0]
    return pl.pallas_call(
        merge_kernel,
        in_specs=[
            pl.BlockSpec(memory_space=pltpu.SMEM),
            pl.BlockSpec(memory_space=pltpu.VMEM),
        ],
        out_specs=pl.BlockSpec(memory_space=pltpu.VMEM),
        scratch_shapes=[pltpu.VMEM((peers * 33, LANES), f32)],
        out_shape=jax.ShapeDtypeStruct((peers, 32, LANES), bf16),
        compiler_params=pltpu.CompilerParams(vmem_limit_bytes=VMEM_LIMIT),
        name="merge_rows",
    )(me, x)


def split3(x):
    a = x.astype(bf16)
    rest = x - a.astype(f32)
    b = rest.astype(bf16)
    return a, b, (rest - b.astype(f32)).astype(bf16)


def coarse_kernel(
    z_ref, basis_ref, rows_ref, owned_hbm, top_ref, flat, applied, owned_ref, sems
):
    slots, width, coarse = basis_ref.shape
    half = slots // 2
    rows = z_ref.shape[1]
    step = rows + 1
    left, d, keep = masks()
    eye = d == 0
    for j in range(Q):
        flat[step * j : step * j + rows, :] = z_ref[j].astype(f32)
    for q in range(half):
        f_both = flat[pl.ds(slots * 2 + q, Q, stride=step), :]
        f_turned = f_both.T
        moved = pltpu.roll(f_both, Q - 1, 0)
        for r in (q, q + half):
            t0 = flat[pl.ds(r, Q, stride=step), :]
            t1 = flat[pl.ds(slots + r, Q, stride=step), :]
            turned = jnp.concatenate([t0, t1], axis=0).T
            lower = turned[Q:]
            if r == q:
                f, f_t, d2_diag = f_both, f_turned[:Q], swap_halves(moved)
            else:
                f, f_t, d2_diag = swap_halves(f_both), f_turned[Q:], moved
            d1 = swap_halves(jnp.where(keep, t1, lower))
            d2 = jnp.where(eye, d2_diag, jnp.where(keep, lower, t1))
            d3 = jnp.where(keep[:, :Q], f[:, :Q], f_t)
            owned_ref[r, :Q, :LANES] = jnp.where(left, d1, t0).astype(bf16)
            owned_ref[r, :Q, LANES:] = t0[:, :Q].astype(bf16)
            owned_ref[r, Q : 2 * Q, :LANES] = jnp.where(left, lower, d2).astype(bf16)
            owned_ref[r, Q : 2 * Q, LANES:] = t1[:, :Q].astype(bf16)
            owned_ref[r, 2 * Q :, :LANES] = turned[:Q].astype(bf16)
            owned_ref[r, 2 * Q :, LANES:] = d3.astype(bf16)
    copies = [
        pltpu.make_async_copy(owned_ref.at[r], owned_hbm.at[r], sems.at[r])
        for r in range(slots)
    ]
    for copy in copies:
        copy.start()
    for r in range(slots):
        applied[r] = jnp.dot(
            owned_ref[r], basis_ref[r], preferred_element_type=f32
        ).astype(bf16)
    local_coarse = jnp.dot(
        basis_ref[...].reshape(slots * width, coarse).T,
        applied[...].reshape(slots * width, coarse),
        preferred_element_type=f32,
    )
    rows_t = rows_ref[...]
    inner = 0.0
    for part in split3(local_coarse):
        inner += lax.dot_general(
            part, rows_t, (((1,), (1,)), ((), ())), preferred_element_type=f32
        )
    upper = lower = 0.0
    for part in split3(inner):
        upper += jnp.dot(rows_t[:LANES], part, preferred_element_type=f32)
        lower += jnp.dot(rows_t[LANES:], part[:, LANES:], preferred_element_type=f32)
    top_ref[:LANES, :] = upper[:, :LANES]
    top_ref[LANES : 2 * LANES, :] = upper[:, LANES:]
    top_ref[2 * LANES :, :] = lower
    for copy in copies:
        copy.wait()


def owned_and_top(z, basis, rows_t):
    slots, width, coarse = basis.shape
    vmem = pl.BlockSpec(memory_space=pltpu.VMEM)
    return pl.pallas_call(
        coarse_kernel,
        in_specs=[vmem] * 3,
        out_specs=[pl.BlockSpec(memory_space=pltpu.HBM), vmem],
        scratch_shapes=[
            pltpu.VMEM((Q * (z.shape[1] + 1), LANES), f32),
            pltpu.VMEM((slots, width, coarse), bf16),
            pltpu.VMEM((slots, width, width), bf16),
            pltpu.SemaphoreType.DMA((slots,)),
        ],
        out_shape=[
            jax.ShapeDtypeStruct((slots, width, width), bf16),
            jax.ShapeDtypeStruct((3 * LANES, LANES), f32),
        ],
        compiler_params=pltpu.CompilerParams(vmem_limit_bytes=VMEM_LIMIT),
        name="owned_and_top",
    )(z, basis, rows_t)


def mirror_kernel(x_ref, out_ref):
    mid = x_ref[LANES : 2 * LANES, :]
    out_ref[:LANES, :LANES] = x_ref[:LANES, :]
    out_ref[:LANES, LANES:] = mid
    out_ref[LANES:, :LANES] = mid.T
    out_ref[LANES:, LANES:] = x_ref[2 * LANES :, :]


def mirror(x):
    return pl.pallas_call(
        mirror_kernel,
        in_specs=[pl.BlockSpec(memory_space=pltpu.VMEM)],
        out_specs=pl.BlockSpec(memory_space=pltpu.VMEM),
        out_shape=jax.ShapeDtypeStruct((2 * LANES, 2 * LANES), f32),
        compiler_params=pltpu.CompilerParams(vmem_limit_bytes=VMEM_LIMIT),
        name="mirror",
    )(x)


def exchange(x, axis, members=None):
    return lax.all_to_all(
        x, axis, split_axis=0, concat_axis=0, tiled=True, axis_index_groups=members
    )


def sum_over_all(x, axes):
    peers, groups = (lax.axis_size(a) for a in axes[::-1])
    near = 16
    near_members = [[k * near + i for i in range(near)] for k in range(peers // near)]
    far_members = [
        list(range(i, peers * groups, near)) for i in range(near)
    ]
    far = peers * groups // near
    rows = x.shape[0] // near
    x = x.reshape(near, rows, LANES).astype(bf16)
    x = jnp.sum(exchange(x, "sub", near_members).astype(f32), axis=0).astype(bf16)
    x = exchange(jnp.broadcast_to(x, (far, rows, LANES)), axes, far_members)
    x = jnp.sum(x.astype(f32), axis=0).astype(f32)
    x = exchange(jnp.broadcast_to(x, (near, rows, LANES)), "sub", near_members)
    return x.reshape(near * rows, LANES).astype(f32)


def local(
    coupling,
    factors,
    face_diag,
    face_block,
    face_owner,
    owner_slot,
    coarse_basis,
    coarse_index,
    projection,
):
    me = lax.axis_index("sub").astype(i32).reshape(1)
    x = pack_faces(face_block, face_owner[:, 0], owner_slot, coupling, factors, face_diag)
    x = exchange(x, "sub")
    group_size = projection.shape[0]
    z = exchange(merge_rows(me, x), "sub")
    z, coarse_index = lax.optimization_barrier((z, coarse_index))
    placement = (coarse_index[:, None] == lax.iota(i32, group_size)[None, :]).astype(bf16)
    rows_t = lax.dot_general(
        projection, placement, (((0,), (1,)), ((), ())), preferred_element_type=f32
    ).astype(bf16)
    owned, top = owned_and_top(z, coarse_basis, rows_t)
    return owned, mirror(sum_over_all(top, ("grp", "sub")))


def solution(mesh):
    return jax.shard_map(
        local,
        mesh=mesh,
        in_specs=(
            P(("grp", "sub"), None, None),
            P(("grp", "sub"), None, None),
            P(("grp", "sub"), None),
            P(("grp", "sub")),
            P(("grp", "sub"), None),
            P(("grp", "sub")),
            P(("grp", "sub"), None, None),
            P(("grp", "sub")),
            P("grp", None),
        ),
        out_specs=(P(("grp", "sub"), None, None), P()),
        check_vma=False,
    )
```

```python
import jax
import jax.numpy as jnp
from jax import lax
from jax.experimental import pallas as pl
from jax.experimental.pallas import tpu as pltpu
from jax.sharding import PartitionSpec as P

Q = 64
LANES = 128
STEP_FACES = 16
KEEP, OWNER_AT, SLOT_AT = 63, 61, 60
PACK_VMEM = 56 * 1024 * 1024
VMEM_LIMIT = 16 * 1024 * 1024
f32, bf16, i32 = jnp.float32, jnp.bfloat16, jnp.int32


def masks():
    row = lax.broadcasted_iota(i32, (Q, LANES), 0)
    lane = lax.broadcasted_iota(i32, (Q, LANES), 1)
    d = ((lane & (Q - 1)) - row) & (Q - 1)
    keep = (d < Q // 2) | ((d == Q // 2) & (row < Q // 2))
    return lane < Q, d, keep


def swap_halves(x):
    return pltpu.roll(x, Q, 1)


def schur_kernel(
    block_hbm,
    owner_hbm,
    slot_hbm,
    coupling_hbm,
    factors_hbm,
    diag_hbm,
    out_ref,
    scratch,
    coupling_ref,
    factors_ref,
    diag_ref,
    block_ref,
    owner_ref,
    slot_ref,
    sems,
):
    faces = coupling_ref.shape[0]
    steps = faces // STEP_FACES
    pairs = faces // 2
    copies = [
        pltpu.make_async_copy(block_hbm, block_ref, sems.at[0]),
        pltpu.make_async_copy(factors_hbm, factors_ref, sems.at[1]),
    ]
    for s in range(steps):
        part = pl.ds(s * STEP_FACES, STEP_FACES)
        copies.append(
            pltpu.make_async_copy(
                coupling_hbm.at[part], coupling_ref.at[part], sems.at[2 + s]
            )
        )
    copies += [
        pltpu.make_async_copy(diag_hbm, diag_ref, sems.at[2 + steps]),
        pltpu.make_async_copy(owner_hbm, owner_ref, sems.at[3 + steps]),
        pltpu.make_async_copy(slot_hbm, slot_ref, sems.at[4 + steps]),
    ]
    for copy in copies:
        copy.start()
    left, d, keep = masks()
    eye = d == 0
    eye_right = eye & ~left
    copies[0].wait()
    copies[1].wait()
    for s in range(steps):
        copies[2 + s].wait()
        interiors = []
        for face in range(s * STEP_FACES, (s + 1) * STEP_FACES):
            c = coupling_ref[face]
            mid = c[:, Q : 2 * Q]
            columns = jnp.concatenate([c[:, 2 * Q :], mid, mid, c[:, :Q]], axis=1)
            interiors.append(
                jnp.dot(
                    factors_ref[block_ref[face]], columns, preferred_element_type=f32
                ).astype(bf16)
            )
        grams = [
            lax.dot_general(x, x, (((0,), (0,)), ((), ())), preferred_element_type=f32)
            for x in interiors
        ]
        if s == 0:
            for copy in copies[-3:]:
                copy.wait()
        last = None
        for q, g in enumerate(grams):
            face = s * STEP_FACES + q
            d3, r1 = g[:Q, :LANES], g[Q : 2 * Q, :LANES]
            t0, d1 = g[3 * Q :, :LANES], g[3 * Q :, LANES:]
            diag01 = diag_ref[face : face + 1, :LANES]
            diag2 = jnp.concatenate([diag_ref[face : face + 1, LANES:]] * 2, axis=1)
            diag10 = swap_halves(diag01)
            t1 = jnp.where(eye_right, diag10, 0.0) - jnp.where(
                left | ~keep, r1, d1
            )
            r2 = g[Q : 2 * Q, LANES:]
            d2_diag = diag10 - pltpu.roll(r2, 1, 0)
            spare = jnp.where(
                d == KEEP,
                d2_diag,
                jnp.where(
                    d == OWNER_AT,
                    owner_ref[face].astype(f32),
                    jnp.where(d == SLOT_AT, slot_ref[face].astype(f32), 0.0),
                ),
            )
            f = jnp.where(keep, jnp.where(eye, diag2, 0.0) - d3, spare)

            def put(k, value):
                scratch[pl.ds(k * Q * (pairs + 1) + face // 2, Q, stride=pairs + 1), :] = value

            odd = face % 2
            put(2 * odd, -t0)
            put(2 * odd + 1, t1)
            if odd:
                put(4, jnp.where(left, last, swap_halves(f)))
            last = f
    for k in range(5):
        for j in range(Q):
            at = Q * (pairs + 1) * k + (pairs + 1) * j
            out_ref[j, pairs * k : pairs * (k + 1), :] = scratch[at : at + pairs, :].astype(bf16)


def pack_faces(face_block, owner, slot, coupling, factors, face_diag):
    faces = coupling.shape[0]
    pairs = faces // 2
    return pl.pallas_call(
        schur_kernel,
        in_specs=[pl.BlockSpec(memory_space=pl.ANY)] * 6,
        out_specs=pl.BlockSpec(memory_space=pltpu.VMEM),
        scratch_shapes=[
            pltpu.VMEM((5 * Q * (pairs + 1), LANES), f32),
            pltpu.VMEM(coupling.shape, bf16),
            pltpu.VMEM(factors.shape, bf16),
            pltpu.VMEM(face_diag.shape, f32),
            pltpu.SMEM((faces,), i32),
            pltpu.SMEM((faces,), i32),
            pltpu.SMEM((faces,), i32),
            pltpu.SemaphoreType.DMA((5 + faces // STEP_FACES,)),
        ],
        out_shape=jax.ShapeDtypeStruct((Q, 5 * pairs, LANES), bf16),
        compiler_params=pltpu.CompilerParams(vmem_limit_bytes=PACK_VMEM),
        name="pack_faces",
    )(face_block, owner, slot, coupling, factors, face_diag)


def merge_kernel(me_ref, x_ref, out_ref, flat):
    peers, rows, _ = x_ref.shape
    pairs = rows // 5
    total = peers * pairs
    slots = 12
    me = me_ref[0]

    def piece(k):
        return x_ref[:, pairs * k : pairs * (k + 1), :].reshape(total, LANES)

    shared = piece(4)
    which = lax.broadcasted_iota(i32, (8, LANES), 0)
    lane = lax.broadcasted_iota(i32, (8, LANES), 1)
    place = ((me + jnp.where((which & 1) == 0, OWNER_AT, SLOT_AT)) & (Q - 1)) + jnp.where(
        which < 2, 0, Q
    )
    pick = ((lane == place) & (which < 4)).astype(f32).astype(bf16)
    named = lax.dot_general(
        pick, shared, (((1,), (1,)), ((), ())), preferred_element_type=f32
    ).astype(i32)
    owners = lax.broadcasted_iota(i32, (peers, total), 0)
    hots = []
    for k in range(2):
        owner_hot = (owners == named[2 * k : 2 * k + 1]).astype(f32).astype(bf16)
        slot = named[2 * k + 1 : 2 * k + 2]
        hots.append(
            jnp.concatenate(
                [owner_hot * (slot == s).astype(f32).astype(bf16) for s in range(slots)],
                axis=0,
            )
        )
    even, odd = hots
    both = jnp.dot(
        even, jnp.concatenate([piece(0), piece(1)], axis=1), preferred_element_type=f32
    ) + jnp.dot(
        odd, jnp.concatenate([piece(2), piece(3)], axis=1), preferred_element_type=f32
    )
    sums = [both[:, :LANES], both[:, LANES:]]
    low = jnp.dot(even, shared, preferred_element_type=f32)
    high = jnp.dot(odd, shared, preferred_element_type=f32)
    half = slots // 2
    first = half * peers
    left = lax.broadcasted_iota(i32, (first, LANES), 1) < Q
    sums.append(
        jnp.where(
            left,
            low[:first] + swap_halves(high[:first]),
            swap_halves(low[first:]) + high[first:],
        )
    )
    out_rows = out_ref.shape[1]
    for k in range(3):
        for s in range(sums[k].shape[0] // peers):
            flat[pl.ds(slots * k + s, peers, stride=out_rows + 1), :] = sums[k][
                peers * s : peers * (s + 1), :
            ]
    for s in range(slots * 2 + half, out_rows):
        flat[pl.ds(s, peers, stride=out_rows + 1), :] = jnp.zeros((peers, LANES), f32)
    for j in range(peers):
        at = (out_rows + 1) * j
        out_ref[j] = flat[at : at + out_rows, :].astype(bf16)


def merge_rows(me, x):
    peers = x.shape[0]
    return pl.pallas_call(
        merge_kernel,
        in_specs=[
            pl.BlockSpec(memory_space=pltpu.SMEM),
            pl.BlockSpec(memory_space=pltpu.VMEM),
        ],
        out_specs=pl.BlockSpec(memory_space=pltpu.VMEM),
        scratch_shapes=[pltpu.VMEM((peers * 33, LANES), f32)],
        out_shape=jax.ShapeDtypeStruct((peers, 32, LANES), bf16),
        compiler_params=pltpu.CompilerParams(vmem_limit_bytes=VMEM_LIMIT),
        name="merge_rows",
    )(me, x)


def split3(x):
    a = x.astype(bf16)
    rest = x - a.astype(f32)
    b = rest.astype(bf16)
    return a, b, (rest - b.astype(f32)).astype(bf16)


def coarse_kernel(
    z_ref, basis_ref, rows_ref, owned_hbm, top_ref, flat, applied, owned_ref, sems
):
    slots, width, coarse = basis_ref.shape
    half = slots // 2
    rows = z_ref.shape[1]
    step = rows + 1
    left, d, keep = masks()
    eye = d == 0
    for j in range(Q):
        flat[step * j : step * j + rows, :] = z_ref[j].astype(f32)
    for q in range(half):
        f_both = flat[pl.ds(slots * 2 + q, Q, stride=step), :]
        f_turned = f_both.T
        moved = pltpu.roll(f_both, Q - 1, 0)
        for r in (q, q + half):
            t0 = flat[pl.ds(r, Q, stride=step), :]
            t1 = flat[pl.ds(slots + r, Q, stride=step), :]
            turned = jnp.concatenate([t0, t1], axis=0).T
            lower = turned[Q:]
            if r == q:
                f, f_t, d2_diag = f_both, f_turned[:Q], swap_halves(moved)
            else:
                f, f_t, d2_diag = swap_halves(f_both), f_turned[Q:], moved
            d1 = swap_halves(jnp.where(keep, t1, lower))
            d2 = jnp.where(eye, d2_diag, jnp.where(keep, lower, t1))
            d3 = jnp.where(keep[:, :Q], f[:, :Q], f_t)
            owned_ref[r, :Q, :LANES] = jnp.where(left, d1, t0).astype(bf16)
            owned_ref[r, :Q, LANES:] = t0[:, :Q].astype(bf16)
            owned_ref[r, Q : 2 * Q, :LANES] = jnp.where(left, lower, d2).astype(bf16)
            owned_ref[r, Q : 2 * Q, LANES:] = t1[:, :Q].astype(bf16)
            owned_ref[r, 2 * Q :, :LANES] = turned[:Q].astype(bf16)
            owned_ref[r, 2 * Q :, LANES:] = d3.astype(bf16)
    copies = [
        pltpu.make_async_copy(owned_ref.at[r], owned_hbm.at[r], sems.at[r])
        for r in range(slots)
    ]
    for copy in copies:
        copy.start()
    for r in range(slots):
        applied[r] = jnp.dot(
            owned_ref[r], basis_ref[r], preferred_element_type=f32
        ).astype(bf16)
    local_coarse = jnp.dot(
        basis_ref[...].reshape(slots * width, coarse).T,
        applied[...].reshape(slots * width, coarse),
        preferred_element_type=f32,
    )
    rows_t = rows_ref[...]
    inner = 0.0
    for part in split3(local_coarse):
        inner += lax.dot_general(
            part, rows_t, (((1,), (1,)), ((), ())), preferred_element_type=f32
        )
    upper = lower = 0.0
    for part in split3(inner):
        upper += jnp.dot(rows_t[:LANES], part, preferred_element_type=f32)
        lower += jnp.dot(rows_t[LANES:], part[:, LANES:], preferred_element_type=f32)
    top_ref[:LANES, :] = upper[:, :LANES]
    top_ref[LANES : 2 * LANES, :] = upper[:, LANES:]
    top_ref[2 * LANES :, :] = lower
    for copy in copies:
        copy.wait()


def owned_and_top(z, basis, rows_t):
    slots, width, coarse = basis.shape
    vmem = pl.BlockSpec(memory_space=pltpu.VMEM)
    return pl.pallas_call(
        coarse_kernel,
        in_specs=[vmem] * 3,
        out_specs=[pl.BlockSpec(memory_space=pltpu.HBM), vmem],
        scratch_shapes=[
            pltpu.VMEM((Q * (z.shape[1] + 1), LANES), f32),
            pltpu.VMEM((slots, width, coarse), bf16),
            pltpu.VMEM((slots, width, width), bf16),
            pltpu.SemaphoreType.DMA((slots,)),
        ],
        out_shape=[
            jax.ShapeDtypeStruct((slots, width, width), bf16),
            jax.ShapeDtypeStruct((3 * LANES, LANES), f32),
        ],
        compiler_params=pltpu.CompilerParams(vmem_limit_bytes=VMEM_LIMIT),
        name="owned_and_top",
    )(z, basis, rows_t)


def mirror_kernel(x_ref, out_ref):
    mid = x_ref[LANES : 2 * LANES, :]
    out_ref[:LANES, :LANES] = x_ref[:LANES, :]
    out_ref[:LANES, LANES:] = mid
    out_ref[LANES:, :LANES] = mid.T
    out_ref[LANES:, LANES:] = x_ref[2 * LANES :, :]


def mirror(x):
    return pl.pallas_call(
        mirror_kernel,
        in_specs=[pl.BlockSpec(memory_space=pltpu.VMEM)],
        out_specs=pl.BlockSpec(memory_space=pltpu.VMEM),
        out_shape=jax.ShapeDtypeStruct((2 * LANES, 2 * LANES), f32),
        compiler_params=pltpu.CompilerParams(vmem_limit_bytes=VMEM_LIMIT),
        name="mirror",
    )(x)


def exchange(x, axis, members=None):
    return lax.all_to_all(
        x, axis, split_axis=0, concat_axis=0, tiled=True, axis_index_groups=members
    )


def sum_over_all(x, axes):
    peers, groups = (lax.axis_size(a) for a in axes[::-1])
    near = 16
    near_members = [[k * near + i for i in range(near)] for k in range(peers // near)]
    far_members = [
        list(range(i, peers * groups, near)) for i in range(near)
    ]
    far = peers * groups // near
    rows = x.shape[0] // near
    x = x.reshape(near, rows, LANES).astype(bf16)
    x = jnp.sum(exchange(x, "sub", near_members).astype(f32), axis=0).astype(bf16)
    x = exchange(jnp.broadcast_to(x, (far, rows, LANES)), axes, far_members)
    x = jnp.sum(x.astype(f32), axis=0).astype(bf16)
    x = exchange(jnp.broadcast_to(x, (near, rows, LANES)), "sub", near_members)
    return x.reshape(near * rows, LANES).astype(f32)


def local(
    coupling,
    factors,
    face_diag,
    face_block,
    face_owner,
    owner_slot,
    coarse_basis,
    coarse_index,
    projection,
):
    me = lax.axis_index("sub").astype(i32).reshape(1)
    x = pack_faces(face_block, face_owner[:, 0], owner_slot, coupling, factors, face_diag)
    x = exchange(x, "sub")
    group_size = projection.shape[0]
    placement = (coarse_index[:, None] == lax.iota(i32, group_size)[None, :]).astype(bf16)
    rows_t = lax.dot_general(
        projection, placement, (((0,), (1,)), ((), ())), preferred_element_type=f32
    ).astype(bf16)
    x, rows_t = lax.optimization_barrier((x, rows_t))
    z = exchange(merge_rows(me, x), "sub")
    owned, top = owned_and_top(z, coarse_basis, rows_t)
    return owned, mirror(sum_over_all(top, ("grp", "sub")))


def solution(mesh):
    return jax.shard_map(
        local,
        mesh=mesh,
        in_specs=(
            P(("grp", "sub"), None, None),
            P(("grp", "sub"), None, None),
            P(("grp", "sub"), None),
            P(("grp", "sub")),
            P(("grp", "sub"), None),
            P(("grp", "sub")),
            P(("grp", "sub"), None, None),
            P(("grp", "sub")),
            P("grp", None),
        ),
        out_specs=(P(("grp", "sub"), None, None), P()),
        check_vma=False,
    )
```

```python
import jax
import jax.numpy as jnp
from jax import lax
from jax.experimental import pallas as pl
from jax.experimental.pallas import tpu as pltpu
from jax.sharding import PartitionSpec as P

Q = 64
LANES = 128
STEP_FACES = 16
KEEP, OWNER_AT, SLOT_AT = 63, 61, 60
PACK_VMEM = 56 * 1024 * 1024
VMEM_LIMIT = 16 * 1024 * 1024
f32, bf16, i32 = jnp.float32, jnp.bfloat16, jnp.int32


def masks():
    row = lax.broadcasted_iota(i32, (Q, LANES), 0)
    lane = lax.broadcasted_iota(i32, (Q, LANES), 1)
    d = ((lane & (Q - 1)) - row) & (Q - 1)
    keep = (d < Q // 2) | ((d == Q // 2) & (row < Q // 2))
    return lane < Q, d, keep


def swap_halves(x):
    return pltpu.roll(x, Q, 1)


def schur_kernel(
    block_hbm,
    owner_hbm,
    slot_hbm,
    coupling_hbm,
    factors_hbm,
    diag_hbm,
    out_ref,
    scratch,
    coupling_ref,
    factors_ref,
    diag_ref,
    block_ref,
    owner_ref,
    slot_ref,
    sems,
):
    faces = coupling_ref.shape[0]
    steps = faces // STEP_FACES
    pairs = faces // 2
    copies = [
        pltpu.make_async_copy(block_hbm, block_ref, sems.at[0]),
        pltpu.make_async_copy(factors_hbm, factors_ref, sems.at[1]),
    ]
    for s in range(steps):
        part = pl.ds(s * STEP_FACES, STEP_FACES)
        copies.append(
            pltpu.make_async_copy(
                coupling_hbm.at[part], coupling_ref.at[part], sems.at[2 + s]
            )
        )
    copies += [
        pltpu.make_async_copy(diag_hbm, diag_ref, sems.at[2 + steps]),
        pltpu.make_async_copy(owner_hbm, owner_ref, sems.at[3 + steps]),
        pltpu.make_async_copy(slot_hbm, slot_ref, sems.at[4 + steps]),
    ]
    for copy in copies:
        copy.start()
    left, d, keep = masks()
    eye = d == 0
    eye_right = eye & ~left
    copies[0].wait()
    copies[1].wait()
    for s in range(steps):
        copies[2 + s].wait()
        interiors = []
        for face in range(s * STEP_FACES, (s + 1) * STEP_FACES):
            c = coupling_ref[face]
            mid = c[:, Q : 2 * Q]
            columns = jnp.concatenate([c[:, 2 * Q :], mid, mid, c[:, :Q]], axis=1)
            interiors.append(
                jnp.dot(
                    factors_ref[block_ref[face]], columns, preferred_element_type=f32
                ).astype(bf16)
            )
        grams = [
            lax.dot_general(x, x, (((0,), (0,)), ((), ())), preferred_element_type=f32)
            for x in interiors
        ]
        if s == 0:
            for copy in copies[-3:]:
                copy.wait()
        last = None
        for q, g in enumerate(grams):
            face = s * STEP_FACES + q
            d3, r1 = g[:Q, :LANES], g[Q : 2 * Q, :LANES]
            t0, d1 = g[3 * Q :, :LANES], g[3 * Q :, LANES:]
            diag01 = diag_ref[face : face + 1, :LANES]
            diag2 = jnp.concatenate([diag_ref[face : face + 1, LANES:]] * 2, axis=1)
            diag10 = swap_halves(diag01)
            t1 = jnp.where(eye_right, diag10, 0.0) - jnp.where(
                left | ~keep, r1, d1
            )
            r2 = g[Q : 2 * Q, LANES:]
            d2_diag = diag10 - pltpu.roll(r2, 1, 0)
            spare = jnp.where(
                d == KEEP,
                d2_diag,
                jnp.where(
                    d == OWNER_AT,
                    owner_ref[face].astype(f32),
                    jnp.where(d == SLOT_AT, slot_ref[face].astype(f32), 0.0),
                ),
            )
            f = jnp.where(keep, jnp.where(eye, diag2, 0.0) - d3, spare)

            def put(k, value):
                scratch[pl.ds(k * Q * (pairs + 1) + face // 2, Q, stride=pairs + 1), :] = value

            odd = face % 2
            put(2 * odd, -t0)
            put(2 * odd + 1, t1)
            if odd:
                put(4, jnp.where(left, last, swap_halves(f)))
            last = f
    for k in range(5):
        for j in range(Q):
            at = Q * (pairs + 1) * k + (pairs + 1) * j
            out_ref[j, pairs * k : pairs * (k + 1), :] = scratch[at : at + pairs, :].astype(bf16)


def pack_faces(face_block, owner, slot, coupling, factors, face_diag):
    faces = coupling.shape[0]
    pairs = faces // 2
    return pl.pallas_call(
        schur_kernel,
        in_specs=[pl.BlockSpec(memory_space=pl.ANY)] * 6,
        out_specs=pl.BlockSpec(memory_space=pltpu.VMEM),
        scratch_shapes=[
            pltpu.VMEM(((5 * Q + 1) * (pairs + 1), LANES), f32),
            pltpu.VMEM(coupling.shape, bf16),
            pltpu.VMEM(factors.shape, bf16),
            pltpu.VMEM(face_diag.shape, f32),
            pltpu.SMEM((faces,), i32),
            pltpu.SMEM((faces,), i32),
            pltpu.SMEM((faces,), i32),
            pltpu.SemaphoreType.DMA((5 + faces // STEP_FACES,)),
        ],
        out_shape=jax.ShapeDtypeStruct((Q, 5 * pairs, LANES), bf16),
        compiler_params=pltpu.CompilerParams(vmem_limit_bytes=PACK_VMEM),
        name="pack_faces",
    )(face_block, owner, slot, coupling, factors, face_diag)


def merge_kernel(me_ref, x_ref, out_ref, flat):
    peers, rows, _ = x_ref.shape
    pairs = rows // 5
    total = peers * pairs
    slots = 12
    me = me_ref[0]

    def piece(k):
        return x_ref[:, pairs * k : pairs * (k + 1), :].reshape(total, LANES)

    shared = piece(4)
    which = lax.broadcasted_iota(i32, (8, LANES), 0)
    lane = lax.broadcasted_iota(i32, (8, LANES), 1)
    place = ((me + jnp.where((which & 1) == 0, OWNER_AT, SLOT_AT)) & (Q - 1)) + jnp.where(
        which < 2, 0, Q
    )
    pick = ((lane == place) & (which < 4)).astype(f32).astype(bf16)
    named = lax.dot_general(
        pick, shared, (((1,), (1,)), ((), ())), preferred_element_type=f32
    ).astype(i32)
    owners = lax.broadcasted_iota(i32, (peers, total), 0)
    hots = []
    for k in range(2):
        owner_hot = (owners == named[2 * k : 2 * k + 1]).astype(f32).astype(bf16)
        slot = named[2 * k + 1 : 2 * k + 2]
        hots.append(
            jnp.concatenate(
                [owner_hot * (slot == s).astype(f32).astype(bf16) for s in range(slots)],
                axis=0,
            )
        )
    even, odd = hots
    both = jnp.dot(
        even, jnp.concatenate([piece(0), piece(1)], axis=1), preferred_element_type=f32
    ) + jnp.dot(
        odd, jnp.concatenate([piece(2), piece(3)], axis=1), preferred_element_type=f32
    )
    sums = [both[:, :LANES], both[:, LANES:]]
    low = jnp.dot(even, shared, preferred_element_type=f32)
    high = jnp.dot(odd, shared, preferred_element_type=f32)
    half = slots // 2
    first = half * peers
    left = lax.broadcasted_iota(i32, (first, LANES), 1) < Q
    sums.append(
        jnp.where(
            left,
            low[:first] + swap_halves(high[:first]),
            swap_halves(low[first:]) + high[first:],
        )
    )
    out_rows = out_ref.shape[1]
    for k in range(3):
        for s in range(sums[k].shape[0] // peers):
            flat[pl.ds(slots * k + s, peers, stride=out_rows + 1), :] = sums[k][
                peers * s : peers * (s + 1), :
            ]
    for s in range(slots * 2 + half, out_rows):
        flat[pl.ds(s, peers, stride=out_rows + 1), :] = jnp.zeros((peers, LANES), f32)
    for j in range(peers):
        at = (out_rows + 1) * j
        out_ref[j] = flat[at : at + out_rows, :].astype(bf16)


def merge_rows(me, x):
    peers = x.shape[0]
    return pl.pallas_call(
        merge_kernel,
        in_specs=[
            pl.BlockSpec(memory_space=pltpu.SMEM),
            pl.BlockSpec(memory_space=pltpu.VMEM),
        ],
        out_specs=pl.BlockSpec(memory_space=pltpu.VMEM),
        scratch_shapes=[pltpu.VMEM(((peers + 1) * 33, LANES), f32)],
        out_shape=jax.ShapeDtypeStruct((peers, 32, LANES), bf16),
        compiler_params=pltpu.CompilerParams(vmem_limit_bytes=VMEM_LIMIT),
        name="merge_rows",
    )(me, x)


def split3(x):
    a = x.astype(bf16)
    rest = x - a.astype(f32)
    b = rest.astype(bf16)
    return a, b, (rest - b.astype(f32)).astype(bf16)


def coarse_kernel(
    z_ref, basis_ref, rows_ref, owned_hbm, top_ref, flat, applied, owned_ref, sems
):
    slots, width, coarse = basis_ref.shape
    half = slots // 2
    rows = z_ref.shape[1]
    step = rows + 1
    left, d, keep = masks()
    eye = d == 0
    for j in range(Q):
        flat[step * j : step * j + rows, :] = z_ref[j].astype(f32)
    for q in range(half):
        f_both = flat[pl.ds(slots * 2 + q, Q, stride=step), :]
        f_turned = f_both.T
        moved = pltpu.roll(f_both, Q - 1, 0)
        for r in (q, q + half):
            t0 = flat[pl.ds(r, Q, stride=step), :]
            t1 = flat[pl.ds(slots + r, Q, stride=step), :]
            turned = jnp.concatenate([t0, t1], axis=0).T
            lower = turned[Q:]
            if r == q:
                f, f_t, d2_diag = f_both, f_turned[:Q], swap_halves(moved)
            else:
                f, f_t, d2_diag = swap_halves(f_both), f_turned[Q:], moved
            d1 = swap_halves(jnp.where(keep, t1, lower))
            d2 = jnp.where(eye, d2_diag, jnp.where(keep, lower, t1))
            d3 = jnp.where(keep[:, :Q], f[:, :Q], f_t)
            owned_ref[r, :Q, :LANES] = jnp.where(left, d1, t0).astype(bf16)
            owned_ref[r, :Q, LANES:] = t0[:, :Q].astype(bf16)
            owned_ref[r, Q : 2 * Q, :LANES] = jnp.where(left, lower, d2).astype(bf16)
            owned_ref[r, Q : 2 * Q, LANES:] = t1[:, :Q].astype(bf16)
            owned_ref[r, 2 * Q :, :LANES] = turned[:Q].astype(bf16)
            owned_ref[r, 2 * Q :, LANES:] = d3.astype(bf16)
    copies = [
        pltpu.make_async_copy(owned_ref.at[r], owned_hbm.at[r], sems.at[r])
        for r in range(slots)
    ]
    for copy in copies:
        copy.start()
    for r in range(slots):
        applied[r] = jnp.dot(
            owned_ref[r], basis_ref[r], preferred_element_type=f32
        ).astype(bf16)
    local_coarse = jnp.dot(
        basis_ref[...].reshape(slots * width, coarse).T,
        applied[...].reshape(slots * width, coarse),
        preferred_element_type=f32,
    )
    rows_t = rows_ref[...]
    inner = 0.0
    for part in split3(local_coarse):
        inner += lax.dot_general(
            part, rows_t, (((1,), (1,)), ((), ())), preferred_element_type=f32
        )
    upper = lower = 0.0
    for part in split3(inner):
        upper += jnp.dot(rows_t[:LANES], part, preferred_element_type=f32)
        lower += jnp.dot(rows_t[LANES:], part[:, LANES:], preferred_element_type=f32)
    top_ref[:LANES, :] = upper[:, :LANES]
    top_ref[LANES : 2 * LANES, :] = upper[:, LANES:]
    top_ref[2 * LANES :, :] = lower
    for copy in copies:
        copy.wait()


def owned_and_top(z, basis, rows_t):
    slots, width, coarse = basis.shape
    vmem = pl.BlockSpec(memory_space=pltpu.VMEM)
    return pl.pallas_call(
        coarse_kernel,
        in_specs=[vmem] * 3,
        out_specs=[pl.BlockSpec(memory_space=pltpu.HBM), vmem],
        scratch_shapes=[
            pltpu.VMEM(((Q + 1) * (z.shape[1] + 1), LANES), f32),
            pltpu.VMEM((slots, width, coarse), bf16),
            pltpu.VMEM((slots, width, width), bf16),
            pltpu.SemaphoreType.DMA((slots,)),
        ],
        out_shape=[
            jax.ShapeDtypeStruct((slots, width, width), bf16),
            jax.ShapeDtypeStruct((3 * LANES, LANES), f32),
        ],
        compiler_params=pltpu.CompilerParams(vmem_limit_bytes=VMEM_LIMIT),
        name="owned_and_top",
    )(z, basis, rows_t)


def mirror_kernel(x_ref, out_ref):
    mid = x_ref[LANES : 2 * LANES, :]
    out_ref[:LANES, :LANES] = x_ref[:LANES, :]
    out_ref[:LANES, LANES:] = mid
    out_ref[LANES:, :LANES] = mid.T
    out_ref[LANES:, LANES:] = x_ref[2 * LANES :, :]


def mirror(x):
    return pl.pallas_call(
        mirror_kernel,
        in_specs=[pl.BlockSpec(memory_space=pltpu.VMEM)],
        out_specs=pl.BlockSpec(memory_space=pltpu.VMEM),
        out_shape=jax.ShapeDtypeStruct((2 * LANES, 2 * LANES), f32),
        compiler_params=pltpu.CompilerParams(vmem_limit_bytes=VMEM_LIMIT),
        name="mirror",
    )(x)


def exchange(x, axis, members=None):
    return lax.all_to_all(
        x, axis, split_axis=0, concat_axis=0, tiled=True, axis_index_groups=members
    )


def total(x):
    return lax.optimization_barrier(jnp.sum(x.astype(f32), axis=0)).astype(bf16)


def sum_over_all(x, axes):
    peers, groups = (lax.axis_size(a) for a in axes[::-1])
    near = 16
    near_members = [[k * near + i for i in range(near)] for k in range(peers // near)]
    far_members = [
        list(range(i, peers * groups, near)) for i in range(near)
    ]
    far = peers * groups // near
    rows = x.shape[0] // near
    x = x.reshape(near, rows, LANES).astype(bf16)
    x = total(exchange(x, "sub", near_members))
    x = exchange(jnp.broadcast_to(x, (far, rows, LANES)), axes, far_members)
    x = total(x)
    x = exchange(jnp.broadcast_to(x, (near, rows, LANES)), "sub", near_members)
    return x.reshape(near * rows, LANES).astype(f32)


def local(
    coupling,
    factors,
    face_diag,
    face_block,
    face_owner,
    owner_slot,
    coarse_basis,
    coarse_index,
    projection,
):
    me = lax.axis_index("sub").astype(i32).reshape(1)
    x = pack_faces(face_block, face_owner[:, 0], owner_slot, coupling, factors, face_diag)
    x = exchange(x, "sub")
    group_size = projection.shape[0]
    placement = (coarse_index[:, None] == lax.iota(i32, group_size)[None, :]).astype(bf16)
    rows_t = lax.dot_general(
        projection, placement, (((0,), (1,)), ((), ())), preferred_element_type=f32
    ).astype(bf16)
    x, rows_t = lax.optimization_barrier((x, rows_t))
    z = exchange(merge_rows(me, x), "sub")
    owned, top = owned_and_top(z, coarse_basis, rows_t)
    return owned, mirror(sum_over_all(top, ("grp", "sub")))


def solution(mesh):
    return jax.shard_map(
        local,
        mesh=mesh,
        in_specs=(
            P(("grp", "sub"), None, None),
            P(("grp", "sub"), None, None),
            P(("grp", "sub"), None),
            P(("grp", "sub")),
            P(("grp", "sub"), None),
            P(("grp", "sub")),
            P(("grp", "sub"), None, None),
            P(("grp", "sub")),
            P("grp", None),
        ),
        out_specs=(P(("grp", "sub"), None, None), P()),
        check_vma=False,
    )
```

```python
import jax
import jax.numpy as jnp
from jax import lax
from jax.experimental import pallas as pl
from jax.experimental.pallas import tpu as pltpu
from jax.sharding import PartitionSpec as P

Q = 64
LANES = 128
STEP_FACES = 16
KEEP, OWNER_AT, SLOT_AT = 63, 61, 60
PACK_VMEM = 56 * 1024 * 1024
VMEM_LIMIT = 16 * 1024 * 1024
f32, bf16, i32 = jnp.float32, jnp.bfloat16, jnp.int32


def masks():
    row = lax.broadcasted_iota(i32, (Q, LANES), 0)
    lane = lax.broadcasted_iota(i32, (Q, LANES), 1)
    d = ((lane & (Q - 1)) - row) & (Q - 1)
    keep = (d < Q // 2) | ((d == Q // 2) & (row < Q // 2))
    return lane < Q, d, keep


def swap_halves(x):
    return pltpu.roll(x, Q, 1)


def schur_kernel(
    block_hbm,
    owner_hbm,
    slot_hbm,
    coupling_hbm,
    factors_hbm,
    diag_hbm,
    out_ref,
    scratch,
    coupling_ref,
    factors_ref,
    diag_ref,
    block_ref,
    owner_ref,
    slot_ref,
    sems,
):
    faces = coupling_ref.shape[0]
    steps = faces // STEP_FACES
    pairs = faces // 2
    copies = [
        pltpu.make_async_copy(block_hbm, block_ref, sems.at[0]),
        pltpu.make_async_copy(factors_hbm, factors_ref, sems.at[1]),
    ]
    for s in range(steps):
        part = pl.ds(s * STEP_FACES, STEP_FACES)
        copies.append(
            pltpu.make_async_copy(
                coupling_hbm.at[part], coupling_ref.at[part], sems.at[2 + s]
            )
        )
    copies += [
        pltpu.make_async_copy(diag_hbm, diag_ref, sems.at[2 + steps]),
        pltpu.make_async_copy(owner_hbm, owner_ref, sems.at[3 + steps]),
        pltpu.make_async_copy(slot_hbm, slot_ref, sems.at[4 + steps]),
    ]
    for copy in copies[:2] + copies[-3:] + copies[2:-3]:
        copy.start()
    left, d, keep = masks()
    eye = d == 0
    eye_right = eye & ~left
    for copy in copies[:2] + copies[-3:]:
        copy.wait()
    for s in range(steps):
        copies[2 + s].wait()
        interiors = []
        for face in range(s * STEP_FACES, (s + 1) * STEP_FACES):
            c = coupling_ref[face]
            mid = c[:, Q : 2 * Q]
            columns = jnp.concatenate([c[:, 2 * Q :], mid, mid, c[:, :Q]], axis=1)
            interiors.append(
                jnp.dot(
                    factors_ref[block_ref[face]], columns, preferred_element_type=f32
                ).astype(bf16)
            )
        grams = [
            lax.dot_general(x, x, (((0,), (0,)), ((), ())), preferred_element_type=f32)
            for x in interiors
        ]
        last = None
        for q, g in enumerate(grams):
            face = s * STEP_FACES + q
            d3, r1 = g[:Q, :LANES], g[Q : 2 * Q, :LANES]
            t0, d1 = g[3 * Q :, :LANES], g[3 * Q :, LANES:]
            diag01 = diag_ref[face : face + 1, :LANES]
            diag2 = jnp.concatenate([diag_ref[face : face + 1, LANES:]] * 2, axis=1)
            diag10 = swap_halves(diag01)
            t1 = jnp.where(eye_right, diag10, 0.0) - jnp.where(
                left | ~keep, r1, d1
            )
            r2 = g[Q : 2 * Q, LANES:]
            d2_diag = diag10 - pltpu.roll(r2, 1, 0)
            spare = jnp.where(
                d == KEEP,
                d2_diag,
                jnp.where(
                    d == OWNER_AT,
                    owner_ref[face].astype(f32),
                    jnp.where(d == SLOT_AT, slot_ref[face].astype(f32), 0.0),
                ),
            )
            f = jnp.where(keep, jnp.where(eye, diag2, 0.0) - d3, spare)

            def put(k, value):
                scratch[pl.ds(k * Q * (pairs + 1) + face // 2, Q, stride=pairs + 1), :] = value

            odd = face % 2
            put(2 * odd, -t0)
            put(2 * odd + 1, t1)
            if odd:
                put(4, jnp.where(left, last, swap_halves(f)))
            last = f
    for k in range(5):
        for j in range(Q):
            at = Q * (pairs + 1) * k + (pairs + 1) * j
            out_ref[j, pairs * k : pairs * (k + 1), :] = scratch[at : at + pairs, :].astype(bf16)


def pack_faces(face_block, owner, slot, coupling, factors, face_diag):
    faces = coupling.shape[0]
    pairs = faces // 2
    return pl.pallas_call(
        schur_kernel,
        in_specs=[pl.BlockSpec(memory_space=pl.ANY)] * 6,
        out_specs=pl.BlockSpec(memory_space=pltpu.VMEM),
        scratch_shapes=[
            pltpu.VMEM(((5 * Q + 1) * (pairs + 1), LANES), f32),
            pltpu.VMEM(coupling.shape, bf16),
            pltpu.VMEM(factors.shape, bf16),
            pltpu.VMEM(face_diag.shape, f32),
            pltpu.SMEM((faces,), i32),
            pltpu.SMEM((faces,), i32),
            pltpu.SMEM((faces,), i32),
            pltpu.SemaphoreType.DMA((5 + faces // STEP_FACES,)),
        ],
        out_shape=jax.ShapeDtypeStruct((Q, 5 * pairs, LANES), bf16),
        compiler_params=pltpu.CompilerParams(vmem_limit_bytes=PACK_VMEM),
        name="pack_faces",
    )(face_block, owner, slot, coupling, factors, face_diag)


def merge_kernel(me_ref, x_ref, out_ref, flat):
    peers, rows, _ = x_ref.shape
    pairs = rows // 5
    total = peers * pairs
    slots = 12
    me = me_ref[0]

    def piece(k):
        return x_ref[:, pairs * k : pairs * (k + 1), :].reshape(total, LANES)

    shared = piece(4)
    which = lax.broadcasted_iota(i32, (8, LANES), 0)
    lane = lax.broadcasted_iota(i32, (8, LANES), 1)
    place = ((me + jnp.where((which & 1) == 0, OWNER_AT, SLOT_AT)) & (Q - 1)) + jnp.where(
        which < 2, 0, Q
    )
    pick = ((lane == place) & (which < 4)).astype(f32).astype(bf16)
    named = lax.dot_general(
        pick, shared, (((1,), (1,)), ((), ())), preferred_element_type=f32
    ).astype(i32)
    owners = lax.broadcasted_iota(i32, (peers, total), 0)
    hots = []
    for k in range(2):
        owner_hot = (owners == named[2 * k : 2 * k + 1]).astype(f32).astype(bf16)
        slot = named[2 * k + 1 : 2 * k + 2]
        hots.append(
            jnp.concatenate(
                [owner_hot * (slot == s).astype(f32).astype(bf16) for s in range(slots)],
                axis=0,
            )
        )
    even, odd = hots
    both = jnp.dot(
        even, jnp.concatenate([piece(0), piece(1)], axis=1), preferred_element_type=f32
    ) + jnp.dot(
        odd, jnp.concatenate([piece(2), piece(3)], axis=1), preferred_element_type=f32
    )
    sums = [both[:, :LANES], both[:, LANES:]]
    low = jnp.dot(even, shared, preferred_element_type=f32)
    high = jnp.dot(odd, shared, preferred_element_type=f32)
    half = slots // 2
    first = half * peers
    left = lax.broadcasted_iota(i32, (first, LANES), 1) < Q
    sums.append(
        jnp.where(
            left,
            low[:first] + swap_halves(high[:first]),
            swap_halves(low[first:]) + high[first:],
        )
    )
    out_rows = out_ref.shape[1]
    for k in range(3):
        for s in range(sums[k].shape[0] // peers):
            flat[pl.ds(slots * k + s, peers, stride=out_rows + 1), :] = sums[k][
                peers * s : peers * (s + 1), :
            ]
    for s in range(slots * 2 + half, out_rows):
        flat[pl.ds(s, peers, stride=out_rows + 1), :] = jnp.zeros((peers, LANES), f32)
    for j in range(peers):
        at = (out_rows + 1) * j
        out_ref[j] = flat[at : at + out_rows, :].astype(bf16)


def merge_rows(me, x):
    peers = x.shape[0]
    return pl.pallas_call(
        merge_kernel,
        in_specs=[
            pl.BlockSpec(memory_space=pltpu.SMEM),
            pl.BlockSpec(memory_space=pltpu.VMEM),
        ],
        out_specs=pl.BlockSpec(memory_space=pltpu.VMEM),
        scratch_shapes=[pltpu.VMEM(((peers + 1) * 33, LANES), f32)],
        out_shape=jax.ShapeDtypeStruct((peers, 32, LANES), bf16),
        compiler_params=pltpu.CompilerParams(vmem_limit_bytes=VMEM_LIMIT),
        name="merge_rows",
    )(me, x)


def split3(x):
    a = x.astype(bf16)
    rest = x - a.astype(f32)
    b = rest.astype(bf16)
    return a, b, (rest - b.astype(f32)).astype(bf16)


def coarse_kernel(
    z_ref, basis_ref, rows_ref, owned_hbm, top_ref, flat, applied, owned_ref, sems
):
    slots, width, coarse = basis_ref.shape
    half = slots // 2
    rows = z_ref.shape[1]
    step = rows + 1
    left, d, keep = masks()
    eye = d == 0
    for j in range(Q):
        flat[step * j : step * j + rows, :] = z_ref[j].astype(f32)
    copies = [
        pltpu.make_async_copy(owned_ref.at[r], owned_hbm.at[r], sems.at[r])
        for r in range(slots)
    ]
    for q in range(half):
        f_both = flat[pl.ds(slots * 2 + q, Q, stride=step), :]
        f_turned = f_both.T
        moved = pltpu.roll(f_both, Q - 1, 0)
        for r in (q, q + half):
            t0 = flat[pl.ds(r, Q, stride=step), :]
            t1 = flat[pl.ds(slots + r, Q, stride=step), :]
            turned = jnp.concatenate([t0, t1], axis=0).T
            lower = turned[Q:]
            if r == q:
                f, f_t, d2_diag = f_both, f_turned[:Q], swap_halves(moved)
            else:
                f, f_t, d2_diag = swap_halves(f_both), f_turned[Q:], moved
            d1 = swap_halves(jnp.where(keep, t1, lower))
            d2 = jnp.where(eye, d2_diag, jnp.where(keep, lower, t1))
            d3 = jnp.where(keep[:, :Q], f[:, :Q], f_t)
            owned_ref[r, :Q, :LANES] = jnp.where(left, d1, t0).astype(bf16)
            owned_ref[r, :Q, LANES:] = t0[:, :Q].astype(bf16)
            owned_ref[r, Q : 2 * Q, :LANES] = jnp.where(left, lower, d2).astype(bf16)
            owned_ref[r, Q : 2 * Q, LANES:] = t1[:, :Q].astype(bf16)
            owned_ref[r, 2 * Q :, :LANES] = turned[:Q].astype(bf16)
            owned_ref[r, 2 * Q :, LANES:] = d3.astype(bf16)
            copies[r].start()
    for r in range(slots):
        applied[r] = jnp.dot(
            owned_ref[r], basis_ref[r], preferred_element_type=f32
        ).astype(bf16)
    local_coarse = jnp.dot(
        basis_ref[...].reshape(slots * width, coarse).T,
        applied[...].reshape(slots * width, coarse),
        preferred_element_type=f32,
    )
    rows_t = rows_ref[...]
    inner = 0.0
    for part in split3(local_coarse):
        inner += lax.dot_general(
            part, rows_t, (((1,), (1,)), ((), ())), preferred_element_type=f32
        )
    upper = lower = 0.0
    for part in split3(inner):
        upper += jnp.dot(rows_t[:LANES], part, preferred_element_type=f32)
        lower += jnp.dot(rows_t[LANES:], part[:, LANES:], preferred_element_type=f32)
    top_ref[:LANES, :] = upper[:, :LANES]
    top_ref[LANES : 2 * LANES, :] = upper[:, LANES:]
    top_ref[2 * LANES :, :] = lower
    for copy in copies:
        copy.wait()


def owned_and_top(z, basis, rows_t):
    slots, width, coarse = basis.shape
    vmem = pl.BlockSpec(memory_space=pltpu.VMEM)
    return pl.pallas_call(
        coarse_kernel,
        in_specs=[vmem] * 3,
        out_specs=[pl.BlockSpec(memory_space=pltpu.HBM), vmem],
        scratch_shapes=[
            pltpu.VMEM(((Q + 1) * (z.shape[1] + 1), LANES), f32),
            pltpu.VMEM((slots, width, coarse), bf16),
            pltpu.VMEM((slots, width, width), bf16),
            pltpu.SemaphoreType.DMA((slots,)),
        ],
        out_shape=[
            jax.ShapeDtypeStruct((slots, width, width), bf16),
            jax.ShapeDtypeStruct((3 * LANES, LANES), f32),
        ],
        compiler_params=pltpu.CompilerParams(vmem_limit_bytes=VMEM_LIMIT),
        name="owned_and_top",
    )(z, basis, rows_t)


def mirror_kernel(x_ref, out_ref):
    mid = x_ref[LANES : 2 * LANES, :]
    out_ref[:LANES, :LANES] = x_ref[:LANES, :]
    out_ref[:LANES, LANES:] = mid
    out_ref[LANES:, :LANES] = mid.T
    out_ref[LANES:, LANES:] = x_ref[2 * LANES :, :]


def mirror(x):
    return pl.pallas_call(
        mirror_kernel,
        in_specs=[pl.BlockSpec(memory_space=pltpu.VMEM)],
        out_specs=pl.BlockSpec(memory_space=pltpu.VMEM),
        out_shape=jax.ShapeDtypeStruct((2 * LANES, 2 * LANES), f32),
        compiler_params=pltpu.CompilerParams(vmem_limit_bytes=VMEM_LIMIT),
        name="mirror",
    )(x)


def exchange(x, axis, members=None):
    return lax.all_to_all(
        x, axis, split_axis=0, concat_axis=0, tiled=True, axis_index_groups=members
    )


def sum_over_all(x, axes):
    peers, groups = (lax.axis_size(a) for a in axes[::-1])
    near = 16
    far = peers * groups // near
    rows = x.shape[0] // near
    near_members = [[k * near + i for i in range(near)] for k in range(peers // near)]
    far_members = [list(range(i, peers * groups, near)) for i in range(near)]
    x = exchange(x.astype(bf16).reshape(near, rows, LANES), axes[1], near_members)
    x = jnp.sum(x.astype(f32), axis=0).astype(bf16)
    x = exchange(jnp.broadcast_to(x, (far, rows, LANES)), axes, far_members)
    x = jnp.sum(x.astype(f32), axis=0)
    x = exchange(jnp.broadcast_to(x, (near, rows, LANES)), axes[1], near_members)
    return x.reshape(near * rows, LANES)


def local(
    coupling,
    factors,
    face_diag,
    face_block,
    face_owner,
    owner_slot,
    coarse_basis,
    coarse_index,
    projection,
):
    me = lax.axis_index("sub").astype(i32).reshape(1)
    x = pack_faces(face_block, face_owner[:, 0], owner_slot, coupling, factors, face_diag)
    x = exchange(x, "sub")
    group_size = projection.shape[0]
    placement = (coarse_index[:, None] == lax.iota(i32, group_size)[None, :]).astype(bf16)
    rows_t = lax.dot_general(
        projection, placement, (((0,), (1,)), ((), ())), preferred_element_type=f32
    ).astype(bf16)
    x, rows_t = lax.optimization_barrier((x, rows_t))
    z = exchange(merge_rows(me, x), "sub")
    owned, top = owned_and_top(z, coarse_basis, rows_t)
    return owned, mirror(sum_over_all(top, ("grp", "sub")))


def solution(mesh):
    return jax.shard_map(
        local,
        mesh=mesh,
        in_specs=(
            P(("grp", "sub"), None, None),
            P(("grp", "sub"), None, None),
            P(("grp", "sub"), None),
            P(("grp", "sub")),
            P(("grp", "sub"), None),
            P(("grp", "sub")),
            P(("grp", "sub"), None, None),
            P(("grp", "sub")),
            P("grp", None),
        ),
        out_specs=(P(("grp", "sub"), None, None), P()),
        check_vma=False,
    )
```

```python
import jax
import jax.numpy as jnp
from jax import lax
from jax.experimental import pallas as pl
from jax.experimental.pallas import tpu as pltpu
from jax.sharding import PartitionSpec as P

Q = 64
LANES = 128
CUTS = (0, 8, 32)
KEEP, OWNER_AT, SLOT_AT = 63, 61, 60
PACK_VMEM = 56 * 1024 * 1024
VMEM_LIMIT = 16 * 1024 * 1024
f32, bf16, i32 = jnp.float32, jnp.bfloat16, jnp.int32


def masks():
    row = lax.broadcasted_iota(i32, (Q, LANES), 0)
    lane = lax.broadcasted_iota(i32, (Q, LANES), 1)
    d = ((lane & (Q - 1)) - row) & (Q - 1)
    keep = (d < Q // 2) | ((d == Q // 2) & (row < Q // 2))
    return lane < Q, d, keep


def swap_halves(x):
    return pltpu.roll(x, Q, 1)


def schur_kernel(
    block_hbm,
    owner_hbm,
    slot_hbm,
    coupling_hbm,
    factors_hbm,
    diag_hbm,
    out_ref,
    scratch,
    coupling_ref,
    factors_ref,
    diag_ref,
    block_ref,
    owner_ref,
    slot_ref,
    sems,
):
    faces = coupling_ref.shape[0]
    steps = len(CUTS) - 1
    pairs = faces // 2
    copies = [
        pltpu.make_async_copy(block_hbm, block_ref, sems.at[0]),
        pltpu.make_async_copy(factors_hbm, factors_ref, sems.at[1]),
    ]
    for s in range(steps):
        part = pl.ds(CUTS[s], CUTS[s + 1] - CUTS[s])
        copies.append(
            pltpu.make_async_copy(
                coupling_hbm.at[part], coupling_ref.at[part], sems.at[2 + s]
            )
        )
    copies += [
        pltpu.make_async_copy(diag_hbm, diag_ref, sems.at[2 + steps]),
        pltpu.make_async_copy(owner_hbm, owner_ref, sems.at[3 + steps]),
        pltpu.make_async_copy(slot_hbm, slot_ref, sems.at[4 + steps]),
    ]
    for copy in copies[:2] + copies[-3:] + copies[2:-3]:
        copy.start()
    left, d, keep = masks()
    eye = d == 0
    eye_right = eye & ~left
    for copy in copies[:2] + copies[-3:]:
        copy.wait()
    for s in range(steps):
        copies[2 + s].wait()
        interiors = []
        for face in range(CUTS[s], CUTS[s + 1]):
            c = coupling_ref[face]
            mid = c[:, Q : 2 * Q]
            columns = jnp.concatenate([c[:, 2 * Q :], mid, mid, c[:, :Q]], axis=1)
            interiors.append(
                jnp.dot(
                    factors_ref[block_ref[face]], columns, preferred_element_type=f32
                ).astype(bf16)
            )
        grams = [
            lax.dot_general(x, x, (((0,), (0,)), ((), ())), preferred_element_type=f32)
            for x in interiors
        ]
        last = None
        for q, g in enumerate(grams):
            face = CUTS[s] + q
            d3, r1 = g[:Q, :LANES], g[Q : 2 * Q, :LANES]
            t0, d1 = g[3 * Q :, :LANES], g[3 * Q :, LANES:]
            diag01 = diag_ref[face : face + 1, :LANES]
            diag2 = jnp.concatenate([diag_ref[face : face + 1, LANES:]] * 2, axis=1)
            diag10 = swap_halves(diag01)
            t1 = jnp.where(eye_right, diag10, 0.0) - jnp.where(
                left | ~keep, r1, d1
            )
            r2 = g[Q : 2 * Q, LANES:]
            d2_diag = diag10 - pltpu.roll(r2, 1, 0)
            spare = jnp.where(
                d == KEEP,
                d2_diag,
                jnp.where(
                    d == OWNER_AT,
                    owner_ref[face].astype(f32),
                    jnp.where(d == SLOT_AT, slot_ref[face].astype(f32), 0.0),
                ),
            )
            f = jnp.where(keep, jnp.where(eye, diag2, 0.0) - d3, spare)

            def put(k, value):
                scratch[pl.ds(k * Q * (pairs + 1) + face // 2, Q, stride=pairs + 1), :] = value

            odd = face % 2
            put(2 * odd, -t0)
            put(2 * odd + 1, t1)
            if odd:
                put(4, jnp.where(left, last, swap_halves(f)))
            last = f
    for k in range(5):
        for j in range(Q):
            at = Q * (pairs + 1) * k + (pairs + 1) * j
            out_ref[j, pairs * k : pairs * (k + 1), :] = scratch[at : at + pairs, :].astype(bf16)


def pack_faces(face_block, owner, slot, coupling, factors, face_diag):
    faces = coupling.shape[0]
    pairs = faces // 2
    return pl.pallas_call(
        schur_kernel,
        in_specs=[pl.BlockSpec(memory_space=pl.ANY)] * 6,
        out_specs=pl.BlockSpec(memory_space=pltpu.VMEM),
        scratch_shapes=[
            pltpu.VMEM(((5 * Q + 1) * (pairs + 1), LANES), f32),
            pltpu.VMEM(coupling.shape, bf16),
            pltpu.VMEM(factors.shape, bf16),
            pltpu.VMEM(face_diag.shape, f32),
            pltpu.SMEM((faces,), i32),
            pltpu.SMEM((faces,), i32),
            pltpu.SMEM((faces,), i32),
            pltpu.SemaphoreType.DMA((4 + len(CUTS),)),
        ],
        out_shape=jax.ShapeDtypeStruct((Q, 5 * pairs, LANES), bf16),
        compiler_params=pltpu.CompilerParams(vmem_limit_bytes=PACK_VMEM),
        name="pack_faces",
    )(face_block, owner, slot, coupling, factors, face_diag)


def merge_kernel(me_ref, x_ref, out_ref, flat):
    peers, rows, _ = x_ref.shape
    pairs = rows // 5
    total = peers * pairs
    slots = 12
    me = me_ref[0]

    def piece(k):
        return x_ref[:, pairs * k : pairs * (k + 1), :].reshape(total, LANES)

    shared = piece(4)
    which = lax.broadcasted_iota(i32, (8, LANES), 0)
    lane = lax.broadcasted_iota(i32, (8, LANES), 1)
    place = ((me + jnp.where((which & 1) == 0, OWNER_AT, SLOT_AT)) & (Q - 1)) + jnp.where(
        which < 2, 0, Q
    )
    pick = ((lane == place) & (which < 4)).astype(f32).astype(bf16)
    named = lax.dot_general(
        pick, shared, (((1,), (1,)), ((), ())), preferred_element_type=f32
    ).astype(i32)
    owners = lax.broadcasted_iota(i32, (peers, total), 0)
    hots = []
    for k in range(2):
        owner_hot = (owners == named[2 * k : 2 * k + 1]).astype(f32).astype(bf16)
        slot = named[2 * k + 1 : 2 * k + 2]
        hots.append(
            jnp.concatenate(
                [owner_hot * (slot == s).astype(f32).astype(bf16) for s in range(slots)],
                axis=0,
            )
        )
    even, odd = hots
    both = jnp.dot(
        even, jnp.concatenate([piece(0), piece(1)], axis=1), preferred_element_type=f32
    ) + jnp.dot(
        odd, jnp.concatenate([piece(2), piece(3)], axis=1), preferred_element_type=f32
    )
    sums = [both[:, :LANES], both[:, LANES:]]
    low = jnp.dot(even, shared, preferred_element_type=f32)
    high = jnp.dot(odd, shared, preferred_element_type=f32)
    half = slots // 2
    first = half * peers
    left = lax.broadcasted_iota(i32, (first, LANES), 1) < Q
    sums.append(
        jnp.where(
            left,
            low[:first] + swap_halves(high[:first]),
            swap_halves(low[first:]) + high[first:],
        )
    )
    out_rows = out_ref.shape[1]
    for k in range(3):
        for s in range(sums[k].shape[0] // peers):
            flat[pl.ds(slots * k + s, peers, stride=out_rows + 1), :] = sums[k][
                peers * s : peers * (s + 1), :
            ]
    for s in range(slots * 2 + half, out_rows):
        flat[pl.ds(s, peers, stride=out_rows + 1), :] = jnp.zeros((peers, LANES), f32)
    for j in range(peers):
        at = (out_rows + 1) * j
        out_ref[j] = flat[at : at + out_rows, :].astype(bf16)


def merge_rows(me, x):
    peers = x.shape[0]
    return pl.pallas_call(
        merge_kernel,
        in_specs=[
            pl.BlockSpec(memory_space=pltpu.SMEM),
            pl.BlockSpec(memory_space=pltpu.VMEM),
        ],
        out_specs=pl.BlockSpec(memory_space=pltpu.VMEM),
        scratch_shapes=[pltpu.VMEM(((peers + 1) * 33, LANES), f32)],
        out_shape=jax.ShapeDtypeStruct((peers, 32, LANES), bf16),
        compiler_params=pltpu.CompilerParams(vmem_limit_bytes=VMEM_LIMIT),
        name="merge_rows",
    )(me, x)


def split3(x):
    a = x.astype(bf16)
    rest = x - a.astype(f32)
    b = rest.astype(bf16)
    return a, b, (rest - b.astype(f32)).astype(bf16)


def coarse_kernel(
    z_ref, basis_ref, rows_ref, owned_hbm, top_ref, flat, applied, owned_ref, sems
):
    slots, width, coarse = basis_ref.shape
    half = slots // 2
    rows = z_ref.shape[1]
    step = rows + 1
    left, d, keep = masks()
    eye = d == 0
    for j in range(Q):
        flat[step * j : step * j + rows, :] = z_ref[j].astype(f32)
    copies = [
        pltpu.make_async_copy(owned_ref.at[r], owned_hbm.at[r], sems.at[r])
        for r in range(slots)
    ]
    for q in range(half):
        f_both = flat[pl.ds(slots * 2 + q, Q, stride=step), :]
        f_turned = f_both.T
        moved = pltpu.roll(f_both, Q - 1, 0)
        for r in (q, q + half):
            t0 = flat[pl.ds(r, Q, stride=step), :]
            t1 = flat[pl.ds(slots + r, Q, stride=step), :]
            turned = jnp.concatenate([t0, t1], axis=0).T
            lower = turned[Q:]
            if r == q:
                f, f_t, d2_diag = f_both, f_turned[:Q], swap_halves(moved)
            else:
                f, f_t, d2_diag = swap_halves(f_both), f_turned[Q:], moved
            d1 = swap_halves(jnp.where(keep, t1, lower))
            d2 = jnp.where(eye, d2_diag, jnp.where(keep, lower, t1))
            d3 = jnp.where(keep[:, :Q], f[:, :Q], f_t)
            owned_ref[r, :Q, :LANES] = jnp.where(left, d1, t0).astype(bf16)
            owned_ref[r, :Q, LANES:] = t0[:, :Q].astype(bf16)
            owned_ref[r, Q : 2 * Q, :LANES] = jnp.where(left, lower, d2).astype(bf16)
            owned_ref[r, Q : 2 * Q, LANES:] = t1[:, :Q].astype(bf16)
            owned_ref[r, 2 * Q :, :LANES] = turned[:Q].astype(bf16)
            owned_ref[r, 2 * Q :, LANES:] = d3.astype(bf16)
            copies[r].start()
    for r in range(slots):
        applied[r] = jnp.dot(
            owned_ref[r], basis_ref[r], preferred_element_type=f32
        ).astype(bf16)
    local_coarse = jnp.dot(
        basis_ref[...].reshape(slots * width, coarse).T,
        applied[...].reshape(slots * width, coarse),
        preferred_element_type=f32,
    )
    rows_t = rows_ref[...]
    inner = 0.0
    for part in split3(local_coarse):
        inner += lax.dot_general(
            part, rows_t, (((1,), (1,)), ((), ())), preferred_element_type=f32
        )
    upper = lower = 0.0
    for part in split3(inner):
        upper += jnp.dot(rows_t[:LANES], part, preferred_element_type=f32)
        lower += jnp.dot(rows_t[LANES:], part[:, LANES:], preferred_element_type=f32)
    top_ref[:LANES, :] = upper[:, :LANES]
    top_ref[LANES : 2 * LANES, :] = upper[:, LANES:]
    top_ref[2 * LANES :, :] = lower
    for copy in copies:
        copy.wait()


def owned_and_top(z, basis, rows_t):
    slots, width, coarse = basis.shape
    vmem = pl.BlockSpec(memory_space=pltpu.VMEM)
    return pl.pallas_call(
        coarse_kernel,
        in_specs=[vmem] * 3,
        out_specs=[pl.BlockSpec(memory_space=pltpu.HBM), vmem],
        scratch_shapes=[
            pltpu.VMEM(((Q + 1) * (z.shape[1] + 1), LANES), f32),
            pltpu.VMEM((slots, width, coarse), bf16),
            pltpu.VMEM((slots, width, width), bf16),
            pltpu.SemaphoreType.DMA((slots,)),
        ],
        out_shape=[
            jax.ShapeDtypeStruct((slots, width, width), bf16),
            jax.ShapeDtypeStruct((3 * LANES, LANES), f32),
        ],
        compiler_params=pltpu.CompilerParams(vmem_limit_bytes=VMEM_LIMIT),
        name="owned_and_top",
    )(z, basis, rows_t)


def mirror_kernel(x_ref, out_ref):
    mid = x_ref[LANES : 2 * LANES, :]
    out_ref[:LANES, :LANES] = x_ref[:LANES, :]
    out_ref[:LANES, LANES:] = mid
    out_ref[LANES:, :LANES] = mid.T
    out_ref[LANES:, LANES:] = x_ref[2 * LANES :, :]


def mirror(x):
    return pl.pallas_call(
        mirror_kernel,
        in_specs=[pl.BlockSpec(memory_space=pltpu.VMEM)],
        out_specs=pl.BlockSpec(memory_space=pltpu.VMEM),
        out_shape=jax.ShapeDtypeStruct((2 * LANES, 2 * LANES), f32),
        compiler_params=pltpu.CompilerParams(vmem_limit_bytes=VMEM_LIMIT),
        name="mirror",
    )(x)


def exchange(x, axis, members=None):
    return lax.all_to_all(
        x, axis, split_axis=0, concat_axis=0, tiled=True, axis_index_groups=members
    )


def sum_over_all(x, axes):
    peers, groups = (lax.axis_size(a) for a in axes[::-1])
    near = 16
    far = peers * groups // near
    rows = x.shape[0] // near
    near_members = [[k * near + i for i in range(near)] for k in range(peers // near)]
    far_members = [list(range(i, peers * groups, near)) for i in range(near)]
    x = exchange(x.astype(bf16).reshape(near, rows, LANES), axes[1], near_members)
    x = jnp.sum(x.astype(f32), axis=0).astype(bf16)
    x = exchange(jnp.broadcast_to(x, (far, rows, LANES)), axes, far_members)
    x = jnp.sum(x.astype(f32), axis=0)
    x = exchange(jnp.broadcast_to(x, (near, rows, LANES)), axes[1], near_members)
    return x.reshape(near * rows, LANES)


def local(
    coupling,
    factors,
    face_diag,
    face_block,
    face_owner,
    owner_slot,
    coarse_basis,
    coarse_index,
    projection,
):
    me = lax.axis_index("sub").astype(i32).reshape(1)
    x = pack_faces(face_block, face_owner[:, 0], owner_slot, coupling, factors, face_diag)
    x = exchange(x, "sub")
    group_size = projection.shape[0]
    placement = (coarse_index[:, None] == lax.iota(i32, group_size)[None, :]).astype(bf16)
    rows_t = lax.dot_general(
        projection, placement, (((0,), (1,)), ((), ())), preferred_element_type=f32
    ).astype(bf16)
    x, rows_t = lax.optimization_barrier((x, rows_t))
    z = exchange(merge_rows(me, x), "sub")
    owned, top = owned_and_top(z, coarse_basis, rows_t)
    return owned, mirror(sum_over_all(top, ("grp", "sub")))


def solution(mesh):
    return jax.shard_map(
        local,
        mesh=mesh,
        in_specs=(
            P(("grp", "sub"), None, None),
            P(("grp", "sub"), None, None),
            P(("grp", "sub"), None),
            P(("grp", "sub")),
            P(("grp", "sub"), None),
            P(("grp", "sub")),
            P(("grp", "sub"), None, None),
            P(("grp", "sub")),
            P("grp", None),
        ),
        out_specs=(P(("grp", "sub"), None, None), P()),
        check_vma=False,
    )
```

```python
import jax
import jax.numpy as jnp
from jax import lax
from jax.experimental import pallas as pl
from jax.experimental.pallas import tpu as pltpu
from jax.sharding import PartitionSpec as P

Q = 64
LANES = 128
CUTS = (0, 8, 32)
KEEP, OWNER_AT, SLOT_AT = 63, 61, 60
PACK_VMEM = 56 * 1024 * 1024
VMEM_LIMIT = 16 * 1024 * 1024
f32, bf16, i32 = jnp.float32, jnp.bfloat16, jnp.int32


def masks():
    row = lax.broadcasted_iota(i32, (Q, LANES), 0)
    lane = lax.broadcasted_iota(i32, (Q, LANES), 1)
    d = ((lane & (Q - 1)) - row) & (Q - 1)
    keep = (d < Q // 2) | ((d == Q // 2) & (row < Q // 2))
    return lane < Q, d, keep


def swap_halves(x):
    return pltpu.roll(x, Q, 1)


def schur_kernel(
    block_hbm,
    owner_hbm,
    slot_hbm,
    coupling_hbm,
    factors_hbm,
    diag_hbm,
    out_ref,
    scratch,
    coupling_ref,
    factors_ref,
    diag_ref,
    block_ref,
    owner_ref,
    slot_ref,
    sems,
):
    faces = coupling_ref.shape[0]
    steps = len(CUTS) - 1
    pairs = faces // 2
    copies = [
        pltpu.make_async_copy(block_hbm, block_ref, sems.at[0]),
        pltpu.make_async_copy(factors_hbm, factors_ref, sems.at[1]),
    ]
    for s in range(steps):
        part = pl.ds(CUTS[s], CUTS[s + 1] - CUTS[s])
        copies.append(
            pltpu.make_async_copy(
                coupling_hbm.at[part], coupling_ref.at[part], sems.at[2 + s]
            )
        )
    copies += [
        pltpu.make_async_copy(diag_hbm, diag_ref, sems.at[2 + steps]),
        pltpu.make_async_copy(owner_hbm, owner_ref, sems.at[3 + steps]),
        pltpu.make_async_copy(slot_hbm, slot_ref, sems.at[4 + steps]),
    ]
    for copy in copies[:2] + copies[-3:] + copies[2:-3]:
        copy.start()
    left, d, keep = masks()
    eye = d == 0
    eye_right = eye & ~left
    for copy in copies[:2] + copies[-3:]:
        copy.wait()
    for s in range(steps):
        copies[2 + s].wait()
        interiors = []
        for face in range(CUTS[s], CUTS[s + 1]):
            c = coupling_ref[face]
            mid = c[:, Q : 2 * Q]
            columns = jnp.concatenate([c[:, 2 * Q :], mid, mid, c[:, :Q]], axis=1)
            interiors.append(
                jnp.dot(
                    factors_ref[block_ref[face]], columns, preferred_element_type=f32
                ).astype(bf16)
            )
        grams = [
            lax.dot_general(x, x, (((0,), (0,)), ((), ())), preferred_element_type=f32)
            for x in interiors
        ]
        last = None
        for q, g in enumerate(grams):
            face = CUTS[s] + q
            d3, r1 = g[:Q, :LANES], g[Q : 2 * Q, :LANES]
            t0, d1 = g[3 * Q :, :LANES], g[3 * Q :, LANES:]
            diag01 = diag_ref[face : face + 1, :LANES]
            diag2 = jnp.concatenate([diag_ref[face : face + 1, LANES:]] * 2, axis=1)
            diag10 = swap_halves(diag01)
            t1 = jnp.where(eye_right, diag10, 0.0) - jnp.where(
                left | ~keep, r1, d1
            )
            r2 = g[Q : 2 * Q, LANES:]
            d2_diag = diag10 - pltpu.roll(r2, 1, 0)
            spare = jnp.where(
                d == KEEP,
                d2_diag,
                jnp.where(
                    d == OWNER_AT,
                    owner_ref[face].astype(f32),
                    jnp.where(d == SLOT_AT, slot_ref[face].astype(f32), 0.0),
                ),
            )
            f = jnp.where(keep, jnp.where(eye, diag2, 0.0) - d3, spare)

            def put(k, value):
                scratch[pl.ds(k * Q * (pairs + 1) + face // 2, Q, stride=pairs + 1), :] = value

            odd = face % 2
            put(2 * odd, -t0)
            put(2 * odd + 1, t1)
            if odd:
                put(4, jnp.where(left, last, swap_halves(f)))
            last = f
    for k in range(5):
        for j in range(Q):
            at = Q * (pairs + 1) * k + (pairs + 1) * j
            out_ref[j, pairs * k : pairs * (k + 1), :] = scratch[at : at + pairs, :].astype(bf16)


def pack_faces(face_block, owner, slot, coupling, factors, face_diag):
    faces = coupling.shape[0]
    pairs = faces // 2
    return pl.pallas_call(
        schur_kernel,
        in_specs=[pl.BlockSpec(memory_space=pl.ANY)] * 6,
        out_specs=pl.BlockSpec(memory_space=pltpu.VMEM),
        scratch_shapes=[
            pltpu.VMEM(((5 * Q + 1) * (pairs + 1), LANES), f32),
            pltpu.VMEM(coupling.shape, bf16),
            pltpu.VMEM(factors.shape, bf16),
            pltpu.VMEM(face_diag.shape, f32),
            pltpu.SMEM((faces,), i32),
            pltpu.SMEM((faces,), i32),
            pltpu.SMEM((faces,), i32),
            pltpu.SemaphoreType.DMA((4 + len(CUTS),)),
        ],
        out_shape=jax.ShapeDtypeStruct((Q, 5 * pairs, LANES), bf16),
        compiler_params=pltpu.CompilerParams(vmem_limit_bytes=PACK_VMEM),
        name="pack_faces",
    )(face_block, owner, slot, coupling, factors, face_diag)


def merge_kernel(me_ref, x_ref, out_ref, flat):
    peers, rows, _ = x_ref.shape
    pairs = rows // 5
    total = peers * pairs
    slots = 12
    me = me_ref[0]

    def piece(k):
        return x_ref[:, pairs * k : pairs * (k + 1), :].reshape(total, LANES)

    shared = piece(4)
    which = lax.broadcasted_iota(i32, (8, LANES), 0)
    lane = lax.broadcasted_iota(i32, (8, LANES), 1)
    place = ((me + jnp.where((which & 1) == 0, OWNER_AT, SLOT_AT)) & (Q - 1)) + jnp.where(
        which < 2, 0, Q
    )
    pick = ((lane == place) & (which < 4)).astype(f32).astype(bf16)
    named = lax.dot_general(
        pick, shared, (((1,), (1,)), ((), ())), preferred_element_type=f32
    ).astype(i32)
    owners = lax.broadcasted_iota(i32, (peers, total), 0)
    hots = []
    for k in range(2):
        owner_hot = (owners == named[2 * k : 2 * k + 1]).astype(f32).astype(bf16)
        slot = named[2 * k + 1 : 2 * k + 2]
        hots.append(
            jnp.concatenate(
                [owner_hot * (slot == s).astype(f32).astype(bf16) for s in range(slots)],
                axis=0,
            )
        )
    even, odd = hots
    both = jnp.dot(
        even, jnp.concatenate([piece(0), piece(1)], axis=1), preferred_element_type=f32
    ) + jnp.dot(
        odd, jnp.concatenate([piece(2), piece(3)], axis=1), preferred_element_type=f32
    )
    sums = [both[:, :LANES], both[:, LANES:]]
    low = jnp.dot(even, shared, preferred_element_type=f32)
    high = jnp.dot(odd, shared, preferred_element_type=f32)
    half = slots // 2
    first = half * peers
    left = lax.broadcasted_iota(i32, (first, LANES), 1) < Q
    sums.append(
        jnp.where(
            left,
            low[:first] + swap_halves(high[:first]),
            swap_halves(low[first:]) + high[first:],
        )
    )
    out_rows = out_ref.shape[1]
    for k in range(3):
        for s in range(sums[k].shape[0] // peers):
            flat[pl.ds(slots * k + s, peers, stride=out_rows + 1), :] = sums[k][
                peers * s : peers * (s + 1), :
            ]
    for s in range(slots * 2 + half, out_rows):
        flat[pl.ds(s, peers, stride=out_rows + 1), :] = jnp.zeros((peers, LANES), f32)
    for j in range(peers):
        at = (out_rows + 1) * j
        out_ref[j] = flat[at : at + out_rows, :].astype(bf16)


def merge_rows(me, x):
    peers = x.shape[0]
    return pl.pallas_call(
        merge_kernel,
        in_specs=[
            pl.BlockSpec(memory_space=pltpu.SMEM),
            pl.BlockSpec(memory_space=pltpu.VMEM),
        ],
        out_specs=pl.BlockSpec(memory_space=pltpu.VMEM),
        scratch_shapes=[pltpu.VMEM(((peers + 1) * 33, LANES), f32)],
        out_shape=jax.ShapeDtypeStruct((peers, 32, LANES), bf16),
        compiler_params=pltpu.CompilerParams(vmem_limit_bytes=VMEM_LIMIT),
        name="merge_rows",
    )(me, x)


def split3(x):
    a = x.astype(bf16)
    rest = x - a.astype(f32)
    b = rest.astype(bf16)
    return a, b, (rest - b.astype(f32)).astype(bf16)


def coarse_kernel(
    z_ref, basis_ref, rows_ref, owned_hbm, top_ref, flat, applied, owned_ref, sems
):
    slots, width, coarse = basis_ref.shape
    half = slots // 2
    rows = z_ref.shape[1]
    step = rows + 1
    left, d, keep = masks()
    eye = d == 0
    for j in range(Q):
        flat[step * j : step * j + rows, :] = z_ref[j].astype(f32)
    copies = [
        pltpu.make_async_copy(owned_ref.at[r], owned_hbm.at[r], sems.at[r])
        for r in range(slots)
    ]
    for q in range(half):
        f_both = flat[pl.ds(slots * 2 + q, Q, stride=step), :]
        f_turned = f_both.T
        moved = pltpu.roll(f_both, Q - 1, 0)
        for r in (q, q + half):
            t0 = flat[pl.ds(r, Q, stride=step), :]
            t1 = flat[pl.ds(slots + r, Q, stride=step), :]
            turned = jnp.concatenate([t0, t1], axis=0).T
            lower = turned[Q:]
            if r == q:
                f, f_t, d2_diag = f_both, f_turned[:Q], swap_halves(moved)
            else:
                f, f_t, d2_diag = swap_halves(f_both), f_turned[Q:], moved
            d1 = swap_halves(jnp.where(keep, t1, lower))
            d2 = jnp.where(eye, d2_diag, jnp.where(keep, lower, t1))
            d3 = jnp.where(keep[:, :Q], f[:, :Q], f_t)
            owned_ref[r, :Q, :LANES] = jnp.where(left, d1, t0).astype(bf16)
            owned_ref[r, :Q, LANES:] = t0[:, :Q].astype(bf16)
            owned_ref[r, Q : 2 * Q, :LANES] = jnp.where(left, lower, d2).astype(bf16)
            owned_ref[r, Q : 2 * Q, LANES:] = t1[:, :Q].astype(bf16)
            owned_ref[r, 2 * Q :, :LANES] = turned[:Q].astype(bf16)
            owned_ref[r, 2 * Q :, LANES:] = d3.astype(bf16)
            copies[r].start()
    for r in range(slots):
        applied[r] = jnp.dot(
            owned_ref[r], basis_ref[r], preferred_element_type=f32
        ).astype(bf16)
    local_coarse = jnp.dot(
        basis_ref[...].reshape(slots * width, coarse).T,
        applied[...].reshape(slots * width, coarse),
        preferred_element_type=f32,
    )
    rows_t = rows_ref[...]
    inner = 0.0
    for part in split3(local_coarse):
        inner += lax.dot_general(
            part, rows_t, (((1,), (1,)), ((), ())), preferred_element_type=f32
        )
    upper = lower = 0.0
    for part in split3(inner):
        upper += jnp.dot(rows_t[:LANES], part, preferred_element_type=f32)
        lower += jnp.dot(rows_t[LANES:], part[:, LANES:], preferred_element_type=f32)
    top_ref[:LANES, :] = upper[:, :LANES]
    top_ref[LANES : 2 * LANES, :] = upper[:, LANES:]
    top_ref[2 * LANES :, :] = lower
    for copy in copies:
        copy.wait()


def owned_and_top(z, basis, rows_t):
    slots, width, coarse = basis.shape
    vmem = pl.BlockSpec(memory_space=pltpu.VMEM)
    return pl.pallas_call(
        coarse_kernel,
        in_specs=[vmem] * 3,
        out_specs=[pl.BlockSpec(memory_space=pltpu.HBM), vmem],
        scratch_shapes=[
            pltpu.VMEM(((Q + 1) * (z.shape[1] + 1), LANES), f32),
            pltpu.VMEM((slots, width, coarse), bf16),
            pltpu.VMEM((slots, width, width), bf16),
            pltpu.SemaphoreType.DMA((slots,)),
        ],
        out_shape=[
            jax.ShapeDtypeStruct((slots, width, width), bf16),
            jax.ShapeDtypeStruct((3 * LANES, LANES), f32),
        ],
        compiler_params=pltpu.CompilerParams(vmem_limit_bytes=VMEM_LIMIT),
        name="owned_and_top",
    )(z, basis, rows_t)


def mirror_kernel(x_ref, out_ref):
    mid = x_ref[LANES : 2 * LANES, :]
    out_ref[:LANES, :LANES] = x_ref[:LANES, :]
    out_ref[:LANES, LANES:] = mid
    out_ref[LANES:, :LANES] = mid.T
    out_ref[LANES:, LANES:] = x_ref[2 * LANES :, :]


def mirror(x):
    return pl.pallas_call(
        mirror_kernel,
        in_specs=[pl.BlockSpec(memory_space=pltpu.VMEM)],
        out_specs=pl.BlockSpec(memory_space=pltpu.VMEM),
        out_shape=jax.ShapeDtypeStruct((2 * LANES, 2 * LANES), f32),
        compiler_params=pltpu.CompilerParams(vmem_limit_bytes=VMEM_LIMIT),
        name="mirror",
    )(x)


def exchange(x, axis, members=None):
    return lax.all_to_all(
        x, axis, split_axis=0, concat_axis=0, tiled=True, axis_index_groups=members
    )


def sum_over_all(x, axes):
    peers, groups = (lax.axis_size(a) for a in axes[::-1])
    pn, gn = 8, 2
    near = pn * gn
    far = peers * groups // near
    rows = x.shape[0] // near
    near_members = [
        [(g * gn + i) * peers + p * pn + j for i in range(gn) for j in range(pn)]
        for g in range(groups // gn)
        for p in range(peers // pn)
    ]
    far_members = [list(m) for m in zip(*near_members)]
    x = exchange(x.astype(bf16).reshape(near, rows, LANES), axes, near_members)
    x = jnp.sum(x.astype(f32), axis=0).astype(bf16)
    x = exchange(jnp.broadcast_to(x, (far, rows, LANES)), axes, far_members)
    x = jnp.sum(x.astype(f32), axis=0)
    x = exchange(jnp.broadcast_to(x, (near, rows, LANES)), axes, near_members)
    return x.reshape(near * rows, LANES)


def local(
    coupling,
    factors,
    face_diag,
    face_block,
    face_owner,
    owner_slot,
    coarse_basis,
    coarse_index,
    projection,
):
    me = lax.axis_index("sub").astype(i32).reshape(1)
    x = pack_faces(face_block, face_owner[:, 0], owner_slot, coupling, factors, face_diag)
    x = exchange(x, "sub")
    group_size = projection.shape[0]
    placement = (coarse_index[:, None] == lax.iota(i32, group_size)[None, :]).astype(bf16)
    rows_t = lax.dot_general(
        projection, placement, (((0,), (1,)), ((), ())), preferred_element_type=f32
    ).astype(bf16)
    x, rows_t = lax.optimization_barrier((x, rows_t))
    z = exchange(merge_rows(me, x), "sub")
    owned, top = owned_and_top(z, coarse_basis, rows_t)
    return owned, mirror(sum_over_all(top, ("grp", "sub")))


def solution(mesh):
    return jax.shard_map(
        local,
        mesh=mesh,
        in_specs=(
            P(("grp", "sub"), None, None),
            P(("grp", "sub"), None, None),
            P(("grp", "sub"), None),
            P(("grp", "sub")),
            P(("grp", "sub"), None),
            P(("grp", "sub")),
            P(("grp", "sub"), None, None),
            P(("grp", "sub")),
            P("grp", None),
        ),
        out_specs=(P(("grp", "sub"), None, None), P()),
        check_vma=False,
    )
```

```python
import jax
import jax.numpy as jnp
from jax import lax
from jax.experimental import pallas as pl
from jax.experimental.pallas import tpu as pltpu
from jax.sharding import PartitionSpec as P

Q = 64
LANES = 128
CUTS = (0, 8, 32)
KEEP, OWNER_AT, SLOT_AT = 63, 61, 60
PACK_VMEM = 56 * 1024 * 1024
VMEM_LIMIT = 16 * 1024 * 1024
f32, bf16, i32 = jnp.float32, jnp.bfloat16, jnp.int32


def masks():
    row = lax.broadcasted_iota(i32, (Q, LANES), 0)
    lane = lax.broadcasted_iota(i32, (Q, LANES), 1)
    d = ((lane & (Q - 1)) - row) & (Q - 1)
    keep = (d < Q // 2) | ((d == Q // 2) & (row < Q // 2))
    return lane < Q, d, keep


def swap_halves(x):
    return pltpu.roll(x, Q, 1)


def schur_kernel(
    block_hbm,
    owner_hbm,
    slot_hbm,
    coupling_hbm,
    factors_hbm,
    diag_hbm,
    out_ref,
    scratch,
    coupling_ref,
    factors_ref,
    diag_ref,
    block_ref,
    owner_ref,
    slot_ref,
    sems,
):
    faces = coupling_ref.shape[0]
    steps = len(CUTS) - 1
    pairs = faces // 2
    copies = [
        pltpu.make_async_copy(block_hbm, block_ref, sems.at[0]),
        pltpu.make_async_copy(factors_hbm, factors_ref, sems.at[1]),
    ]
    for s in range(steps):
        part = pl.ds(CUTS[s], CUTS[s + 1] - CUTS[s])
        copies.append(
            pltpu.make_async_copy(
                coupling_hbm.at[part], coupling_ref.at[part], sems.at[2 + s]
            )
        )
    copies += [
        pltpu.make_async_copy(diag_hbm, diag_ref, sems.at[2 + steps]),
        pltpu.make_async_copy(owner_hbm, owner_ref, sems.at[3 + steps]),
        pltpu.make_async_copy(slot_hbm, slot_ref, sems.at[4 + steps]),
    ]
    for copy in copies[:2] + copies[-3:] + copies[2:-3]:
        copy.start()
    left, d, keep = masks()
    eye = d == 0
    eye_right = eye & ~left
    for copy in copies[:2] + copies[-3:]:
        copy.wait()
    for s in range(steps):
        copies[2 + s].wait()
        interiors = []
        for face in range(CUTS[s], CUTS[s + 1]):
            c = coupling_ref[face]
            mid = c[:, Q : 2 * Q]
            columns = jnp.concatenate([c[:, 2 * Q :], mid, mid, c[:, :Q]], axis=1)
            interiors.append(
                jnp.dot(
                    factors_ref[block_ref[face]], columns, preferred_element_type=f32
                ).astype(bf16)
            )
        grams = [
            lax.dot_general(x, x, (((0,), (0,)), ((), ())), preferred_element_type=f32)
            for x in interiors
        ]
        last = None
        for q, g in enumerate(grams):
            face = CUTS[s] + q
            d3, r1 = g[:Q, :LANES], g[Q : 2 * Q, :LANES]
            t0, d1 = g[3 * Q :, :LANES], g[3 * Q :, LANES:]
            diag01 = diag_ref[face : face + 1, :LANES]
            diag2 = jnp.concatenate([diag_ref[face : face + 1, LANES:]] * 2, axis=1)
            diag10 = swap_halves(diag01)
            t1 = jnp.where(eye_right, diag10, 0.0) - jnp.where(
                left | ~keep, r1, d1
            )
            r2 = g[Q : 2 * Q, LANES:]
            d2_diag = diag10 - pltpu.roll(r2, 1, 0)
            spare = jnp.where(
                d == KEEP,
                d2_diag,
                jnp.where(
                    d == OWNER_AT,
                    owner_ref[face].astype(f32),
                    jnp.where(d == SLOT_AT, slot_ref[face].astype(f32), 0.0),
                ),
            )
            f = jnp.where(keep, jnp.where(eye, diag2, 0.0) - d3, spare)

            def put(k, value):
                scratch[pl.ds(k * Q * (pairs + 1) + face // 2, Q, stride=pairs + 1), :] = value

            odd = face % 2
            put(2 * odd, -t0)
            put(2 * odd + 1, t1)
            if odd:
                put(4, jnp.where(left, last, swap_halves(f)))
            last = f
    for k in range(5):
        for j in range(Q):
            at = Q * (pairs + 1) * k + (pairs + 1) * j
            out_ref[j, pairs * k : pairs * (k + 1), :] = scratch[at : at + pairs, :].astype(bf16)


def pack_faces(face_block, owner, slot, coupling, factors, face_diag):
    faces = coupling.shape[0]
    pairs = faces // 2
    return pl.pallas_call(
        schur_kernel,
        in_specs=[pl.BlockSpec(memory_space=pl.ANY)] * 6,
        out_specs=pl.BlockSpec(memory_space=pltpu.VMEM),
        scratch_shapes=[
            pltpu.VMEM(((5 * Q + 1) * (pairs + 1), LANES), f32),
            pltpu.VMEM(coupling.shape, bf16),
            pltpu.VMEM(factors.shape, bf16),
            pltpu.VMEM(face_diag.shape, f32),
            pltpu.SMEM((faces,), i32),
            pltpu.SMEM((faces,), i32),
            pltpu.SMEM((faces,), i32),
            pltpu.SemaphoreType.DMA((4 + len(CUTS),)),
        ],
        out_shape=jax.ShapeDtypeStruct((Q, 5 * pairs, LANES), bf16),
        compiler_params=pltpu.CompilerParams(vmem_limit_bytes=PACK_VMEM),
        name="pack_faces",
    )(face_block, owner, slot, coupling, factors, face_diag)


def merge_kernel(me_ref, x_ref, out_ref, flat):
    peers, rows, _ = x_ref.shape
    pairs = rows // 5
    total = peers * pairs
    slots = 12
    me = me_ref[0]

    def piece(k):
        return x_ref[:, pairs * k : pairs * (k + 1), :].reshape(total, LANES)

    shared = piece(4)
    which = lax.broadcasted_iota(i32, (8, LANES), 0)
    lane = lax.broadcasted_iota(i32, (8, LANES), 1)
    place = ((me + jnp.where((which & 1) == 0, OWNER_AT, SLOT_AT)) & (Q - 1)) + jnp.where(
        which < 2, 0, Q
    )
    pick = ((lane == place) & (which < 4)).astype(f32).astype(bf16)
    named = lax.dot_general(
        pick, shared, (((1,), (1,)), ((), ())), preferred_element_type=f32
    ).astype(i32)
    owners = lax.broadcasted_iota(i32, (peers, total), 0)
    hots = []
    for k in range(2):
        owner_hot = (owners == named[2 * k : 2 * k + 1]).astype(f32).astype(bf16)
        slot = named[2 * k + 1 : 2 * k + 2]
        hots.append(
            jnp.concatenate(
                [owner_hot * (slot == s).astype(f32).astype(bf16) for s in range(slots)],
                axis=0,
            )
        )
    even, odd = hots
    both = jnp.dot(
        even, jnp.concatenate([piece(0), piece(1)], axis=1), preferred_element_type=f32
    ) + jnp.dot(
        odd, jnp.concatenate([piece(2), piece(3)], axis=1), preferred_element_type=f32
    )
    sums = [both[:, :LANES], both[:, LANES:]]
    low = jnp.dot(even, shared, preferred_element_type=f32)
    high = jnp.dot(odd, shared, preferred_element_type=f32)
    half = slots // 2
    first = half * peers
    left = lax.broadcasted_iota(i32, (first, LANES), 1) < Q
    sums.append(
        jnp.where(
            left,
            low[:first] + swap_halves(high[:first]),
            swap_halves(low[first:]) + high[first:],
        )
    )
    out_rows = out_ref.shape[1]
    for k in range(3):
        for s in range(sums[k].shape[0] // peers):
            flat[pl.ds(slots * k + s, peers, stride=out_rows + 1), :] = sums[k][
                peers * s : peers * (s + 1), :
            ]
    for s in range(slots * 2 + half, out_rows):
        flat[pl.ds(s, peers, stride=out_rows + 1), :] = jnp.zeros((peers, LANES), f32)
    for j in range(peers):
        at = (out_rows + 1) * j
        out_ref[j] = flat[at : at + out_rows, :].astype(bf16)


def merge_rows(me, x):
    peers = x.shape[0]
    return pl.pallas_call(
        merge_kernel,
        in_specs=[
            pl.BlockSpec(memory_space=pltpu.SMEM),
            pl.BlockSpec(memory_space=pltpu.VMEM),
        ],
        out_specs=pl.BlockSpec(memory_space=pltpu.VMEM),
        scratch_shapes=[pltpu.VMEM(((peers + 1) * 33, LANES), f32)],
        out_shape=jax.ShapeDtypeStruct((peers, 32, LANES), bf16),
        compiler_params=pltpu.CompilerParams(vmem_limit_bytes=VMEM_LIMIT),
        name="merge_rows",
    )(me, x)


def split3(x):
    a = x.astype(bf16)
    rest = x - a.astype(f32)
    b = rest.astype(bf16)
    return a, b, (rest - b.astype(f32)).astype(bf16)


def coarse_kernel(
    z_ref, basis_ref, rows_ref, owned_hbm, top_ref, flat, applied, owned_ref, sems
):
    slots, width, coarse = basis_ref.shape
    half = slots // 2
    rows = z_ref.shape[1]
    step = rows + 1
    left, d, keep = masks()
    eye = d == 0
    for j in range(Q):
        flat[step * j : step * j + rows, :] = z_ref[j].astype(f32)
    copies = [
        pltpu.make_async_copy(owned_ref.at[r], owned_hbm.at[r], sems.at[r])
        for r in range(slots)
    ]
    for q in range(half):
        f_both = flat[pl.ds(slots * 2 + q, Q, stride=step), :]
        f_turned = f_both.T
        moved = pltpu.roll(f_both, Q - 1, 0)
        for r in (q, q + half):
            t0 = flat[pl.ds(r, Q, stride=step), :]
            t1 = flat[pl.ds(slots + r, Q, stride=step), :]
            turned = jnp.concatenate([t0, t1], axis=0).T
            lower = turned[Q:]
            if r == q:
                f, f_t, d2_diag = f_both, f_turned[:Q], swap_halves(moved)
            else:
                f, f_t, d2_diag = swap_halves(f_both), f_turned[Q:], moved
            d1 = swap_halves(jnp.where(keep, t1, lower))
            d2 = jnp.where(eye, d2_diag, jnp.where(keep, lower, t1))
            d3 = jnp.where(keep[:, :Q], f[:, :Q], f_t)
            owned_ref[r, :Q, :LANES] = jnp.where(left, d1, t0).astype(bf16)
            owned_ref[r, :Q, LANES:] = t0[:, :Q].astype(bf16)
            owned_ref[r, Q : 2 * Q, :LANES] = jnp.where(left, lower, d2).astype(bf16)
            owned_ref[r, Q : 2 * Q, LANES:] = t1[:, :Q].astype(bf16)
            owned_ref[r, 2 * Q :, :LANES] = turned[:Q].astype(bf16)
            owned_ref[r, 2 * Q :, LANES:] = d3.astype(bf16)
            copies[r].start()
    for r in range(slots):
        applied[r] = jnp.dot(
            owned_ref[r], basis_ref[r], preferred_element_type=f32
        ).astype(bf16)
    local_coarse = jnp.dot(
        basis_ref[...].reshape(slots * width, coarse).T,
        applied[...].reshape(slots * width, coarse),
        preferred_element_type=f32,
    )
    rows_t = rows_ref[...]
    inner = 0.0
    for part in split3(local_coarse):
        inner += lax.dot_general(
            part, rows_t, (((1,), (1,)), ((), ())), preferred_element_type=f32
        )
    upper = lower = 0.0
    for part in split3(inner):
        upper += jnp.dot(rows_t[:LANES], part, preferred_element_type=f32)
        lower += jnp.dot(rows_t[LANES:], part[:, LANES:], preferred_element_type=f32)
    top_ref[:LANES, :] = upper[:, :LANES].astype(bf16)
    top_ref[LANES : 2 * LANES, :] = upper[:, LANES:].astype(bf16)
    top_ref[2 * LANES :, :] = lower.astype(bf16)
    for copy in copies:
        copy.wait()


def owned_and_top(z, basis, rows_t):
    slots, width, coarse = basis.shape
    vmem = pl.BlockSpec(memory_space=pltpu.VMEM)
    return pl.pallas_call(
        coarse_kernel,
        in_specs=[vmem] * 3,
        out_specs=[pl.BlockSpec(memory_space=pltpu.HBM), vmem],
        scratch_shapes=[
            pltpu.VMEM(((Q + 1) * (z.shape[1] + 1), LANES), f32),
            pltpu.VMEM((slots, width, coarse), bf16),
            pltpu.VMEM((slots, width, width), bf16),
            pltpu.SemaphoreType.DMA((slots,)),
        ],
        out_shape=[
            jax.ShapeDtypeStruct((slots, width, width), bf16),
            jax.ShapeDtypeStruct((3 * LANES, LANES), bf16),
        ],
        compiler_params=pltpu.CompilerParams(vmem_limit_bytes=VMEM_LIMIT),
        name="owned_and_top",
    )(z, basis, rows_t)


def mirror_kernel(x_ref, out_ref):
    mid = x_ref[LANES : 2 * LANES, :]
    out_ref[:LANES, :LANES] = x_ref[:LANES, :]
    out_ref[:LANES, LANES:] = mid
    out_ref[LANES:, :LANES] = mid.T
    out_ref[LANES:, LANES:] = x_ref[2 * LANES :, :]


def mirror(x):
    return pl.pallas_call(
        mirror_kernel,
        in_specs=[pl.BlockSpec(memory_space=pltpu.VMEM)],
        out_specs=pl.BlockSpec(memory_space=pltpu.VMEM),
        out_shape=jax.ShapeDtypeStruct((2 * LANES, 2 * LANES), f32),
        compiler_params=pltpu.CompilerParams(vmem_limit_bytes=VMEM_LIMIT),
        name="mirror",
    )(x)


def exchange(x, axis, members=None):
    return lax.all_to_all(
        x, axis, split_axis=0, concat_axis=0, tiled=True, axis_index_groups=members
    )


def sum_over_all(x, axes):
    peers, groups = (lax.axis_size(a) for a in axes[::-1])
    near = 16
    far = peers * groups // near
    rows = x.shape[0] // near
    near_members = [[k * near + i for i in range(near)] for k in range(peers // near)]
    far_members = [list(range(i, peers * groups, near)) for i in range(near)]
    x = exchange(x.reshape(near, rows, LANES), axes[1], near_members)
    x = jnp.sum(x.astype(f32), axis=0).astype(bf16)
    x = exchange(jnp.broadcast_to(x, (far, rows, LANES)), axes, far_members)
    x = jnp.sum(x.astype(f32), axis=0)
    x = exchange(jnp.broadcast_to(x, (near, rows, LANES)), axes[1], near_members)
    return x.reshape(near * rows, LANES)


def local(
    coupling,
    factors,
    face_diag,
    face_block,
    face_owner,
    owner_slot,
    coarse_basis,
    coarse_index,
    projection,
):
    me = lax.axis_index("sub").astype(i32).reshape(1)
    x = pack_faces(face_block, face_owner[:, 0], owner_slot, coupling, factors, face_diag)
    x = exchange(x, "sub")
    group_size = projection.shape[0]
    placement = (coarse_index[:, None] == lax.iota(i32, group_size)[None, :]).astype(bf16)
    rows_t = lax.dot_general(
        projection, placement, (((0,), (1,)), ((), ())), preferred_element_type=f32
    ).astype(bf16)
    x, rows_t = lax.optimization_barrier((x, rows_t))
    z = exchange(merge_rows(me, x), "sub")
    owned, top = owned_and_top(z, coarse_basis, rows_t)
    return owned, mirror(sum_over_all(top, ("grp", "sub")))


def solution(mesh):
    return jax.shard_map(
        local,
        mesh=mesh,
        in_specs=(
            P(("grp", "sub"), None, None),
            P(("grp", "sub"), None, None),
            P(("grp", "sub"), None),
            P(("grp", "sub")),
            P(("grp", "sub"), None),
            P(("grp", "sub")),
            P(("grp", "sub"), None, None),
            P(("grp", "sub")),
            P("grp", None),
        ),
        out_specs=(P(("grp", "sub"), None, None), P()),
        check_vma=False,
    )
```

```python
import jax
import jax.numpy as jnp
from jax import lax
from jax.experimental import pallas as pl
from jax.experimental.pallas import tpu as pltpu
from jax.sharding import PartitionSpec as P

Q = 64
LANES = 128
STEP_FACES = 16
KEEP, OWNER_AT, SLOT_AT = 63, 61, 60
PACK_VMEM = 56 * 1024 * 1024
VMEM_LIMIT = 16 * 1024 * 1024
f32, bf16, i32 = jnp.float32, jnp.bfloat16, jnp.int32


def masks():
    row = lax.broadcasted_iota(i32, (Q, LANES), 0)
    lane = lax.broadcasted_iota(i32, (Q, LANES), 1)
    d = ((lane & (Q - 1)) - row) & (Q - 1)
    keep = (d < Q // 2) | ((d == Q // 2) & (row < Q // 2))
    return lane < Q, d, keep


def swap_halves(x):
    return pltpu.roll(x, Q, 1)


def schur_kernel(
    block_hbm,
    owner_hbm,
    slot_hbm,
    coupling_hbm,
    factors_hbm,
    diag_hbm,
    out_ref,
    scratch,
    coupling_ref,
    factors_ref,
    diag_ref,
    block_ref,
    owner_ref,
    slot_ref,
    sems,
):
    faces = coupling_ref.shape[0]
    steps = faces // STEP_FACES
    pairs = faces // 2
    copies = [
        pltpu.make_async_copy(block_hbm, block_ref, sems.at[0]),
        pltpu.make_async_copy(factors_hbm, factors_ref, sems.at[1]),
    ]
    for s in range(steps):
        part = pl.ds(s * STEP_FACES, STEP_FACES)
        copies.append(
            pltpu.make_async_copy(
                coupling_hbm.at[part], coupling_ref.at[part], sems.at[2 + s]
            )
        )
    copies += [
        pltpu.make_async_copy(diag_hbm, diag_ref, sems.at[2 + steps]),
        pltpu.make_async_copy(owner_hbm, owner_ref, sems.at[3 + steps]),
        pltpu.make_async_copy(slot_hbm, slot_ref, sems.at[4 + steps]),
    ]
    for copy in copies[:2] + copies[-3:] + copies[2:-3]:
        copy.start()
    left, d, keep = masks()
    eye = d == 0
    eye_right = eye & ~left
    for copy in copies[:2] + copies[-3:]:
        copy.wait()
    @pl.loop(0, steps)
    def _(s):
        part = pl.ds(s * STEP_FACES, STEP_FACES)
        pltpu.make_async_copy(
            coupling_hbm.at[part], coupling_ref.at[part], sems.at[2 + s]
        ).wait()
        diags = diag_ref[pl.ds(pl.multiple_of(s * STEP_FACES, STEP_FACES), STEP_FACES), :]
        interiors = []
        for q in range(STEP_FACES):
            face = s * STEP_FACES + q
            c = coupling_ref[face]
            mid = c[:, Q : 2 * Q]
            columns = jnp.concatenate([c[:, 2 * Q :], mid, mid, c[:, :Q]], axis=1)
            interiors.append(
                jnp.dot(
                    factors_ref[block_ref[face]], columns, preferred_element_type=f32
                ).astype(bf16)
            )
        grams = [
            lax.dot_general(x, x, (((0,), (0,)), ((), ())), preferred_element_type=f32)
            for x in interiors
        ]
        last = None
        for q, g in enumerate(grams):
            face = s * STEP_FACES + q
            d3, r1 = g[:Q, :LANES], g[Q : 2 * Q, :LANES]
            t0, d1 = g[3 * Q :, :LANES], g[3 * Q :, LANES:]
            diag01 = diags[q : q + 1, :LANES]
            diag2 = jnp.concatenate([diags[q : q + 1, LANES:]] * 2, axis=1)
            diag10 = swap_halves(diag01)
            t1 = jnp.where(eye_right, diag10, 0.0) - jnp.where(
                left | ~keep, r1, d1
            )
            r2 = g[Q : 2 * Q, LANES:]
            d2_diag = diag10 - pltpu.roll(r2, 1, 0)
            spare = jnp.where(
                d == KEEP,
                d2_diag,
                jnp.where(
                    d == OWNER_AT,
                    owner_ref[face].astype(f32),
                    jnp.where(d == SLOT_AT, slot_ref[face].astype(f32), 0.0),
                ),
            )
            f = jnp.where(keep, jnp.where(eye, diag2, 0.0) - d3, spare)

            def put(k, value):
                scratch[pl.ds(k * Q * (pairs + 1) + s * (STEP_FACES // 2) + q // 2, Q, stride=pairs + 1), :] = value

            odd = q % 2
            put(2 * odd, -t0)
            put(2 * odd + 1, t1)
            if odd:
                put(4, jnp.where(left, last, swap_halves(f)))
            last = f
    for k in range(5):
        for j in range(Q):
            at = Q * (pairs + 1) * k + (pairs + 1) * j
            out_ref[j, pairs * k : pairs * (k + 1), :] = scratch[at : at + pairs, :].astype(bf16)


def pack_faces(face_block, owner, slot, coupling, factors, face_diag):
    faces = coupling.shape[0]
    pairs = faces // 2
    return pl.pallas_call(
        schur_kernel,
        in_specs=[pl.BlockSpec(memory_space=pl.ANY)] * 6,
        out_specs=pl.BlockSpec(memory_space=pltpu.VMEM),
        scratch_shapes=[
            pltpu.VMEM(((5 * Q + 1) * (pairs + 1), LANES), f32),
            pltpu.VMEM(coupling.shape, bf16),
            pltpu.VMEM(factors.shape, bf16),
            pltpu.VMEM(face_diag.shape, f32),
            pltpu.SMEM((faces,), i32),
            pltpu.SMEM((faces,), i32),
            pltpu.SMEM((faces,), i32),
            pltpu.SemaphoreType.DMA((5 + faces // STEP_FACES,)),
        ],
        out_shape=jax.ShapeDtypeStruct((Q, 5 * pairs, LANES), bf16),
        compiler_params=pltpu.CompilerParams(vmem_limit_bytes=PACK_VMEM),
        name="pack_faces",
    )(face_block, owner, slot, coupling, factors, face_diag)


def merge_kernel(me_ref, x_ref, out_ref, flat):
    peers, rows, _ = x_ref.shape
    pairs = rows // 5
    total = peers * pairs
    slots = 12
    me = me_ref[0]

    def piece(k):
        return x_ref[:, pairs * k : pairs * (k + 1), :].reshape(total, LANES)

    shared = piece(4)
    which = lax.broadcasted_iota(i32, (8, LANES), 0)
    lane = lax.broadcasted_iota(i32, (8, LANES), 1)
    place = ((me + jnp.where((which & 1) == 0, OWNER_AT, SLOT_AT)) & (Q - 1)) + jnp.where(
        which < 2, 0, Q
    )
    pick = ((lane == place) & (which < 4)).astype(f32).astype(bf16)
    named = lax.dot_general(
        pick, shared, (((1,), (1,)), ((), ())), preferred_element_type=f32
    ).astype(i32)
    owners = lax.broadcasted_iota(i32, (peers, total), 0)
    hots = []
    for k in range(2):
        owner_hot = (owners == named[2 * k : 2 * k + 1]).astype(f32).astype(bf16)
        slot = named[2 * k + 1 : 2 * k + 2]
        hots.append(
            jnp.concatenate(
                [owner_hot * (slot == s).astype(f32).astype(bf16) for s in range(slots)],
                axis=0,
            )
        )
    even, odd = hots
    both = jnp.dot(
        even, jnp.concatenate([piece(0), piece(1)], axis=1), preferred_element_type=f32
    ) + jnp.dot(
        odd, jnp.concatenate([piece(2), piece(3)], axis=1), preferred_element_type=f32
    )
    sums = [both[:, :LANES], both[:, LANES:]]
    low = jnp.dot(even, shared, preferred_element_type=f32)
    high = jnp.dot(odd, shared, preferred_element_type=f32)
    half = slots // 2
    first = half * peers
    left = lax.broadcasted_iota(i32, (first, LANES), 1) < Q
    sums.append(
        jnp.where(
            left,
            low[:first] + swap_halves(high[:first]),
            swap_halves(low[first:]) + high[first:],
        )
    )
    out_rows = out_ref.shape[1]
    for k in range(3):
        for s in range(sums[k].shape[0] // peers):
            flat[pl.ds(slots * k + s, peers, stride=out_rows + 1), :] = sums[k][
                peers * s : peers * (s + 1), :
            ]
    for s in range(slots * 2 + half, out_rows):
        flat[pl.ds(s, peers, stride=out_rows + 1), :] = jnp.zeros((peers, LANES), f32)
    for j in range(peers):
        at = (out_rows + 1) * j
        out_ref[j] = flat[at : at + out_rows, :].astype(bf16)


def merge_rows(me, x):
    peers = x.shape[0]
    return pl.pallas_call(
        merge_kernel,
        in_specs=[
            pl.BlockSpec(memory_space=pltpu.SMEM),
            pl.BlockSpec(memory_space=pltpu.VMEM),
        ],
        out_specs=pl.BlockSpec(memory_space=pltpu.VMEM),
        scratch_shapes=[pltpu.VMEM(((peers + 1) * 33, LANES), f32)],
        out_shape=jax.ShapeDtypeStruct((peers, 32, LANES), bf16),
        compiler_params=pltpu.CompilerParams(vmem_limit_bytes=VMEM_LIMIT),
        name="merge_rows",
    )(me, x)


def split3(x):
    a = x.astype(bf16)
    rest = x - a.astype(f32)
    b = rest.astype(bf16)
    return a, b, (rest - b.astype(f32)).astype(bf16)


def coarse_kernel(
    z_ref, basis_ref, rows_ref, owned_hbm, top_ref, flat, applied, owned_ref, sems
):
    slots, width, coarse = basis_ref.shape
    half = slots // 2
    rows = z_ref.shape[1]
    step = rows + 1
    left, d, keep = masks()
    eye = d == 0
    for j in range(Q):
        flat[step * j : step * j + rows, :] = z_ref[j].astype(f32)
    copies = [
        pltpu.make_async_copy(owned_ref.at[r], owned_hbm.at[r], sems.at[r])
        for r in range(slots)
    ]
    for q in range(half):
        f_both = flat[pl.ds(slots * 2 + q, Q, stride=step), :]
        f_turned = f_both.T
        moved = pltpu.roll(f_both, Q - 1, 0)
        for r in (q, q + half):
            t0 = flat[pl.ds(r, Q, stride=step), :]
            t1 = flat[pl.ds(slots + r, Q, stride=step), :]
            turned = jnp.concatenate([t0, t1], axis=0).T
            lower = turned[Q:]
            if r == q:
                f, f_t, d2_diag = f_both, f_turned[:Q], swap_halves(moved)
            else:
                f, f_t, d2_diag = swap_halves(f_both), f_turned[Q:], moved
            d1 = swap_halves(jnp.where(keep, t1, lower))
            d2 = jnp.where(eye, d2_diag, jnp.where(keep, lower, t1))
            d3 = jnp.where(keep[:, :Q], f[:, :Q], f_t)
            owned_ref[r, :Q, :LANES] = jnp.where(left, d1, t0).astype(bf16)
            owned_ref[r, :Q, LANES:] = t0[:, :Q].astype(bf16)
            owned_ref[r, Q : 2 * Q, :LANES] = jnp.where(left, lower, d2).astype(bf16)
            owned_ref[r, Q : 2 * Q, LANES:] = t1[:, :Q].astype(bf16)
            owned_ref[r, 2 * Q :, :LANES] = turned[:Q].astype(bf16)
            owned_ref[r, 2 * Q :, LANES:] = d3.astype(bf16)
            copies[r].start()
    for r in range(slots):
        applied[r] = jnp.dot(
            owned_ref[r], basis_ref[r], preferred_element_type=f32
        ).astype(bf16)
    local_coarse = jnp.dot(
        basis_ref[...].reshape(slots * width, coarse).T,
        applied[...].reshape(slots * width, coarse),
        preferred_element_type=f32,
    )
    rows_t = rows_ref[...]
    inner = 0.0
    for part in split3(local_coarse):
        inner += lax.dot_general(
            part, rows_t, (((1,), (1,)), ((), ())), preferred_element_type=f32
        )
    upper = lower = 0.0
    for part in split3(inner):
        upper += jnp.dot(rows_t[:LANES], part, preferred_element_type=f32)
        lower += jnp.dot(rows_t[LANES:], part[:, LANES:], preferred_element_type=f32)
    top_ref[:LANES, :] = upper[:, :LANES]
    top_ref[LANES : 2 * LANES, :] = upper[:, LANES:]
    top_ref[2 * LANES :, :] = lower
    for copy in copies:
        copy.wait()


def owned_and_top(z, basis, rows_t):
    slots, width, coarse = basis.shape
    vmem = pl.BlockSpec(memory_space=pltpu.VMEM)
    return pl.pallas_call(
        coarse_kernel,
        in_specs=[vmem] * 3,
        out_specs=[pl.BlockSpec(memory_space=pltpu.HBM), vmem],
        scratch_shapes=[
            pltpu.VMEM(((Q + 1) * (z.shape[1] + 1), LANES), f32),
            pltpu.VMEM((slots, width, coarse), bf16),
            pltpu.VMEM((slots, width, width), bf16),
            pltpu.SemaphoreType.DMA((slots,)),
        ],
        out_shape=[
            jax.ShapeDtypeStruct((slots, width, width), bf16),
            jax.ShapeDtypeStruct((3 * LANES, LANES), f32),
        ],
        compiler_params=pltpu.CompilerParams(vmem_limit_bytes=VMEM_LIMIT),
        name="owned_and_top",
    )(z, basis, rows_t)


def mirror_kernel(x_ref, out_ref):
    mid = x_ref[LANES : 2 * LANES, :]
    out_ref[:LANES, :LANES] = x_ref[:LANES, :]
    out_ref[:LANES, LANES:] = mid
    out_ref[LANES:, :LANES] = mid.T
    out_ref[LANES:, LANES:] = x_ref[2 * LANES :, :]


def mirror(x):
    return pl.pallas_call(
        mirror_kernel,
        in_specs=[pl.BlockSpec(memory_space=pltpu.VMEM)],
        out_specs=pl.BlockSpec(memory_space=pltpu.VMEM),
        out_shape=jax.ShapeDtypeStruct((2 * LANES, 2 * LANES), f32),
        compiler_params=pltpu.CompilerParams(vmem_limit_bytes=VMEM_LIMIT),
        name="mirror",
    )(x)


def exchange(x, axis, members=None):
    return lax.all_to_all(
        x, axis, split_axis=0, concat_axis=0, tiled=True, axis_index_groups=members
    )


def sum_over_all(x, axes):
    peers, groups = (lax.axis_size(a) for a in axes[::-1])
    near = 16
    far = peers * groups // near
    rows = x.shape[0] // near
    near_members = [[k * near + i for i in range(near)] for k in range(peers // near)]
    far_members = [list(range(i, peers * groups, near)) for i in range(near)]
    x = exchange(x.astype(bf16).reshape(near, rows, LANES), axes[1], near_members)
    x = jnp.sum(x.astype(f32), axis=0).astype(bf16)
    x = exchange(jnp.broadcast_to(x, (far, rows, LANES)), axes, far_members)
    x = jnp.sum(x.astype(f32), axis=0)
    x = exchange(jnp.broadcast_to(x, (near, rows, LANES)), axes[1], near_members)
    return x.reshape(near * rows, LANES)


def local(
    coupling,
    factors,
    face_diag,
    face_block,
    face_owner,
    owner_slot,
    coarse_basis,
    coarse_index,
    projection,
):
    me = lax.axis_index("sub").astype(i32).reshape(1)
    x = pack_faces(face_block, face_owner[:, 0], owner_slot, coupling, factors, face_diag)
    x = exchange(x, "sub")
    group_size = projection.shape[0]
    placement = (coarse_index[:, None] == lax.iota(i32, group_size)[None, :]).astype(bf16)
    rows_t = lax.dot_general(
        projection, placement, (((0,), (1,)), ((), ())), preferred_element_type=f32
    ).astype(bf16)
    x, rows_t = lax.optimization_barrier((x, rows_t))
    z = exchange(merge_rows(me, x), "sub")
    owned, top = owned_and_top(z, coarse_basis, rows_t)
    return owned, mirror(sum_over_all(top, ("grp", "sub")))


def solution(mesh):
    return jax.shard_map(
        local,
        mesh=mesh,
        in_specs=(
            P(("grp", "sub"), None, None),
            P(("grp", "sub"), None, None),
            P(("grp", "sub"), None),
            P(("grp", "sub")),
            P(("grp", "sub"), None),
            P(("grp", "sub")),
            P(("grp", "sub"), None, None),
            P(("grp", "sub")),
            P("grp", None),
        ),
        out_specs=(P(("grp", "sub"), None, None), P()),
        check_vma=False,
    )
```
